512 devices in a mesh: rows: 32 (over y_lo, z), cols: 16 (over y_hi, x, core).
Axes of the slice: x: 4, y: 4 (y_hi: 2, y_lo: 2; y = y_hi * 2 + y_lo), z: 16, core: 2. Of those that a mesh axis runs over, the one named last changes fastest.
Arguments:
- latent: bfloat16 [256, 64, 1280], P('rows', 'cols'), may hold values from -6 to 6
- ln_gain: float32 [1, 2, 1280], replicated, may hold values from 0.5 to 1.5
- ln_bias: float32 [1, 2, 1280], replicated, may hold values from -3 to 3
- w_qkv: bfloat16 [1, 1024, 3, 1280], P(None, 'cols'), may hold values from -3 to 3
- w_out: bfloat16 [1, 1024, 1280], P(None, 'cols'), may hold values from -0.375 to 0.375
- w_gate: bfloat16 [1, 1280, 5120], P(None, None, 'cols'), may hold values from -0.15625 to 0.15625
- w_value: bfloat16 [1, 1280, 5120], P(None, None, 'cols'), may hold values from -0.15625 to 0.15625
- w_down: bfloat16 [1, 5120, 1280], P(None, 'cols'), may hold values from -0.078125 to 0.078125
Outputs:
- latent_out: bfloat16 [256, 64, 1280], P('rows', 'cols')
The draws below stay inside these ranges and needn't reach their ends.
All inputs are finite; a program needn't handle non-finite values.
Results may differ from the reference program's by a relative error of at most 0.023.
Values may be sent and summed in bfloat16 or wider, within the bound.
A program may use at most 64 MiB of HBM per device.

```python
import jax
import jax.numpy as jnp
from jax import lax

C = 1280
HEADS = 16
HD = 64
FF = 5120
LAYERS = 1
LAT_H = 64
LAT_W = 64
IMAGES = 4
N_COLS = 16


def draw_w_qkv(key, part):
    key = jax.random.fold_in(key, 7)
    first = jax.random.fold_in(key, 0)
    base = jax.random.normal(first, (LAYERS, HEADS * HD, 3, C), jnp.float32) * C ** (-0.5)
    factors = jnp.array([1.5, 1.5, 1.0], jnp.float32).reshape(1, 1, 3, 1)
    base = base * factors
    return jnp.clip(base, -3.0, 3.0).astype(jnp.bfloat16)


def steps_of(own_key, extent, pieces, smallest, high):
    level, own = 1.0, jax.random.fold_in(own_key, 6)
    for position, parts in pieces:
        draws = jnp.exp(jax.random.uniform(jax.random.fold_in(own, position), (parts,), jnp.float32, smallest / len(pieces), high / len(pieces)))
        level = level * jnp.repeat(draws, extent[position] // parts).reshape([-1 if axis == position else 1 for axis in range(len(extent))])
    return level


def scatter_about(stream_key, shape, scale, most, pieces=(), dtype=jnp.bfloat16):
    values = scale * jax.random.normal(stream_key, shape, jnp.float32)
    if pieces:
        values = values * steps_of(stream_key, shape, pieces, -0.22, 0.18)
    return jnp.clip(values, -most, most).astype(dtype)


def setup_inputs(seed: int = 0) -> dict:
    key_list = jax.random.split(jax.random.key(seed), 9)
    latent = scatter_about(key_list[0], (IMAGES * LAT_H, LAT_W, C), 1.0, 6.0, ((0, 32), (1, 16)))
    ln_gain = jnp.clip(1.0 + 0.1 * jax.random.normal(key_list[1], (LAYERS, 2, C), jnp.float32), 0.5, 1.5)
    ln_bias = scatter_about(key_list[2], (LAYERS, 2, C), 0.5, 3.0, (), jnp.float32)
    w_qkv = draw_w_qkv(jax.random.fold_in(key_list[8], 71), 0)
    w_out = scatter_about(key_list[4], (LAYERS, HEADS * HD, C), (HEADS * HD // 4) ** -0.5, 0.375, ((1, 16),))
    w_gate = scatter_about(key_list[5], (LAYERS, C, FF), C ** -0.5, 0.15625, ((2, 16),))
    w_value = scatter_about(key_list[6], (LAYERS, C, FF), C ** -0.5, 0.15625, ((2, 16),))
    w_down = scatter_about(key_list[7], (LAYERS, FF, C), FF ** -0.5, 0.078125, ((1, 16),))
    return {"latent": latent, "ln_gain": ln_gain, "ln_bias": ln_bias, "w_qkv": w_qkv, "w_out": w_out, "w_gate": w_gate, "w_value": w_value, "w_down": w_down}


def norm_rows(stream, ln_gain, ln_bias):
    values = stream.astype(jnp.float32)
    row_mean = lax.optimization_barrier(jnp.mean(values, axis=-1, keepdims=True))
    centred = values - row_mean
    row_var = lax.optimization_barrier(jnp.mean(centred * centred, axis=-1, keepdims=True))
    return (centred * lax.rsqrt(row_var + 1e-05) * ln_gain + ln_bias).astype(jnp.bfloat16)

def grouped_sum(left, right, groups):
    width = left.shape[1] // groups
    total = jnp.zeros((left.shape[0], right.shape[1]), jnp.float32)
    for group in range(groups):
        term = jnp.dot(left[:, group * width:(group + 1) * width], right[group * width:(group + 1) * width], preferred_element_type=jnp.float32)
        rounded = lax.optimization_barrier(term.astype(jnp.bfloat16))
        total = total + rounded.astype(jnp.float32)
    return total

def one_image(stream, ln_gain, ln_bias, w_qkv, w_out, w_gate, w_value, w_down):
    token_count = LAT_H * LAT_W
    score_scale = HD ** (-0.5)
    normed = norm_rows(stream, ln_gain[0], ln_bias[0])
    matrix = jnp.transpose(w_qkv, (2, 1, 0)).reshape(C, 3 * HEADS * HD)
    packed = jnp.dot(normed, matrix, preferred_element_type=jnp.float32).astype(jnp.bfloat16)
    per_head = packed.reshape(token_count, 3, HEADS, HD).transpose(2, 1, 0, 3)

    def one_head(blocks):
        scores = jnp.dot(blocks[0], blocks[1].T, preferred_element_type=jnp.float32) * score_scale
        weights = jnp.exp(scores - lax.optimization_barrier(jnp.max(scores, axis=-1, keepdims=True)))
        mass = lax.optimization_barrier(jnp.sum(weights, axis=-1, keepdims=True))
        return (jnp.dot(weights.astype(jnp.bfloat16), blocks[2], preferred_element_type=jnp.float32) / mass).astype(jnp.bfloat16)
    heads_out = lax.map(one_head, per_head)
    attended = heads_out.transpose(1, 0, 2).reshape(token_count, HEADS * HD)
    attn_sum = grouped_sum(attended, w_out, N_COLS)
    stream = (stream.astype(jnp.float32) + attn_sum).astype(jnp.bfloat16)
    normed_ffn = norm_rows(stream, ln_gain[1], ln_bias[1])
    gate_sum = jnp.dot(normed_ffn, w_gate, preferred_element_type=jnp.float32)
    value_sum = jnp.dot(normed_ffn, w_value, preferred_element_type=jnp.float32)
    hidden = (value_sum * jax.nn.gelu(gate_sum, approximate=False)).astype(jnp.bfloat16)
    ffn_sum = grouped_sum(hidden, w_down, N_COLS)
    return (stream.astype(jnp.float32) + ffn_sum).astype(jnp.bfloat16)

def reference(latent, ln_gain, ln_bias, w_qkv, w_out, w_gate, w_value, w_down):
    images = latent.reshape(IMAGES, LAT_H * LAT_W, C)
    results = []
    for image_index in range(IMAGES):
        stream = images[image_index]
        for level_index in range(LAYERS):
            stream = one_image(stream, ln_gain[level_index], ln_bias[level_index], w_qkv[level_index], w_out[level_index], w_gate[level_index], w_value[level_index], w_down[level_index])
        results.append(stream)
    return jnp.stack(results, axis=0).reshape(IMAGES * LAT_H, LAT_W, C)
```

```python
import math

import jax
import jax.numpy as jnp
from jax import lax
from jax.experimental import pallas as pl
from jax.experimental.pallas import tpu as pltpu
from jax.sharding import PartitionSpec as P

HD = 64
MESH = pl.DeviceIdType.MESH
F32, BF16 = jnp.float32, jnp.bfloat16
ORDERS = ((1, 2, 3, 7, 6, 5, 4), (2, 0, 3, 7, 6, 5, 4), (3, 1, 7, 0, 6, 5, 4), (7, 2, 6, 1, 5, 0, 4))
CODES = [sum(digit * 8**place for place, digit in enumerate(order)) for order in ORDERS]


def norm_rows(values, gain, bias):
    row_mean = jnp.mean(values, axis=-1, keepdims=True)
    centred = values - row_mean
    row_var = jnp.mean(centred * centred, axis=-1, keepdims=True)
    return (centred * lax.rsqrt(row_var + 1e-05) * gain + bias).astype(BF16)


def dot(left, right, left_dim, right_dim):
    return lax.dot_general(
        left, right, (((left_dim,), (right_dim,)), ((), ())), preferred_element_type=F32
    )


def block_kernel(
    latent, gain, bias, w_qkv, w_out, w_gate, w_value, w_down, result,
    gathered, partial, summed, keys, other_keys, query, wkv, wq, wo, wgv, wdown,
    top, accum, attended, attended_other, query_other, hidden,
    sem_w, sem_ws, sem_wr, sem_cs, sem_cr, sem_z, sem_zs, sem_sib, sem_sibs, sem_p, sem_ps,
):
    row, col = lax.axis_index("rows"), lax.axis_index("cols")
    core = col % 2
    place = row % 8
    half = place // 4
    jj = place + half * (7 - 2 * place)
    step = 1 - 2 * half
    inward, outward = row + step, row - step
    entry = row - place + 4 - half
    sibling = (row, col + 1 - 2 * core)
    across = (row + 4 - 8 * half, col)
    mate = lax.bitwise_xor(core, half)

    def chip(distance):
        return (row, lax.bitwise_xor(col, 2 * distance))

    barrier = pltpu.get_barrier_semaphore()
    for distance in range(1, 8):
        pl.semaphore_signal(barrier, inc=1, device_id=chip(distance), device_id_type=MESH)
        pl.semaphore_signal(
            barrier, inc=1, device_id=(lax.bitwise_xor(row, distance), col), device_id_type=MESH
        )
    pl.semaphore_signal(barrier, inc=1, device_id=sibling, device_id_type=MESH)
    pl.semaphore_wait(barrier, 15)

    started = []

    def remote(src, dst, send, recv, device):
        return pltpu.make_async_remote_copy(
            src_ref=src, dst_ref=dst, send_sem=send, recv_sem=recv, device_id=device, device_id_type=MESH
        )

    def begin(*args):
        copy = remote(*args)
        copy.start()
        started.append(copy)
        return copy

    weights = []

    def load_weight(index, src, dst_mine, dst_theirs):
        own = pltpu.make_async_copy(src, dst_mine, sem_w.at[index])
        own.start()
        weights.append((own, begin(src, dst_theirs, sem_ws.at[index], sem_wr.at[index], sibling)))

    load_weight(0, w_qkv.at[pl.ds(HD, 2 * HD)], wkv.at[mate], wkv.at[mate])
    load_weight(1, w_qkv.at[pl.ds(0, HD)], wq.at[mate], wq.at[mate])

    def exchange(buffer, target, first, same):
        copies = []
        for distance in range(1, 8):
            src = buffer.at[0] if same else buffer.at[distance]
            copies.append(
                begin(src, target.at[distance], sem_cs.at[first, distance], sem_cr.at[first, distance], chip(distance))
            )
        return copies

    stream = latent[...].astype(F32)
    gathered[0, 0] = norm_rows(stream, gain[0:1, :], bias[0:1, :])
    copies = exchange(gathered.at[0], gathered.at[0], 0, True)

    load_weight(2, w_out, wo.at[mate], wo.at[mate])
    load_weight(3, w_gate, wgv.at[0], wgv.at[1])
    load_weight(4, w_value, wgv.at[2], wgv.at[3])
    load_weight(5, w_down, wdown.at[0], wdown.at[1])

    for own, sent in weights[:2]:
        own.wait()
        sent.wait_recv()
    for copy in copies:
        copy.wait_recv()

    tokens = gathered[0].reshape(256, -1)
    scale = HD ** (-0.5) * math.log2(math.e)
    queries = (dot(wq[...].reshape(2 * HD, -1), tokens, 1, 1) * scale).astype(BF16)
    query_other[...] = queries[HD:]
    send_query = begin(
        query_other, query.at[pl.ds(0, HD), pl.ds(256, 256)], sem_ps.at[0], sem_p.at[0], across
    )
    packed = dot(tokens, wkv[...].reshape(4 * HD, -1), 1, 1).astype(BF16)
    other_keys[...] = packed[:, 2 * HD :]
    keys[jj, core] = packed[:, : 2 * HD]
    send_foreign = remote(
        other_keys, keys.at[4 + jj, core], sem_ps.at[1], sem_z.at[4 + jj], (entry, col)
    )
    send_foreign.start()
    own_keys = keys.at[jj, core]

    def send_inward(origin, send):
        block = keys.at[origin, core]
        return remote(block, block, send, sem_z.at[origin], (inward, col))

    def send_outward(origin, send):
        block = keys.at[origin, core]
        return remote(block, block, send, sem_z.at[origin], (outward, col))

    def send_sibling(origin):
        block = keys.at[origin, core]
        return remote(block, block, sem_sibs.at[origin], sem_sib.at[origin], sibling)

    def from_sibling(origin):
        block = keys.at[origin, 1 - core]
        return remote(block, block, sem_sibs.at[origin], sem_sib.at[origin], sibling)

    @pl.when(jj >= 1)
    def _():
        send_outward(jj, sem_ps.at[2]).start()

    @pl.when(jj <= 2)
    def _():
        send_inward(jj, sem_ps.at[3]).start()

    send_sibling(jj).start()
    query[0:HD, 0:256] = queries[:HD]
    query[HD:, :] = jnp.zeros((HD, 512), BF16)
    top[...] = jnp.full(top.shape, -1e30, F32)
    accum[...] = jnp.zeros(accum.shape, F32)
    ones_lane = lax.broadcasted_iota(jnp.int32, (512, 2 * HD), 1) < HD

    def fold(origin):
        from_sibling(origin).wait_recv()
        block = keys[origin].reshape(512, 2 * HD)
        scores = dot(block, query[...], 1, 0)
        old = top[...]
        new = jnp.maximum(old, jnp.max(scores, axis=0, keepdims=True))
        weights_ = jnp.exp2(scores - new).astype(BF16)
        values = jnp.where(ones_lane, jnp.ones_like(block), block)
        accum[...] = accum[...] * jnp.exp2(old - new) + dot(values, weights_, 0, 0)
        top[...] = new

    is0 = (1 - jj) * (2 - jj) * (3 - jj) // 6
    is1 = jj * (2 - jj) * (3 - jj) // 2
    is2 = jj * (jj - 1) * (3 - jj) // 2
    is3 = jj * (jj - 1) * (jj - 2) // 6
    code = is0 * CODES[0] + is1 * CODES[1] + is2 * CODES[2] + is3 * CODES[3]

    def one_step(index, carry):
        rest, before = carry
        origin = rest % 8
        send_outward(origin, sem_zs.at[origin]).wait_recv()

        @pl.when(jnp.logical_and(origin > jj, jj >= 1))
        def _():
            send_outward(origin, sem_zs.at[origin]).start()

        @pl.when(jnp.logical_and(origin < jj, jj <= 2))
        def _():
            send_inward(origin, sem_zs.at[origin]).start()

        send_sibling(origin).start()
        fold(before)
        return (rest // 8, origin)

    send_query.wait_recv()
    _, last = lax.fori_loop(0, 7, one_step, (code, jj))
    fold(last)

    def finish_step(origin, carry):
        send_sibling(origin).wait_send()

        @pl.when(
            jnp.logical_or(
                jnp.logical_and(origin > jj, jj >= 1), jnp.logical_and(origin < jj, jj <= 2)
            )
        )
        def _():
            send_outward(origin, sem_zs.at[origin]).wait_send()

        return carry

    final = (accum[HD:, :] / accum[0:1, :]).astype(BF16)
    attended_other[...] = final[:, 256:]
    send_attended = begin(
        attended_other, attended.at[pl.ds(HD, HD)], sem_ps.at[4], sem_p.at[1], across
    )
    attended[0:HD, :] = final[:, :256]
    for own, sent in weights[2:]:
        own.wait()
        sent.wait_recv()
    send_attended.wait_recv()
    partial[0] = (
        dot(attended[...], wo[...].reshape(2 * HD, -1), 0, 0).astype(BF16).reshape(partial.shape[1:])
    )
    copies = exchange(partial.at[0], summed.at[0], 1, False)
    total = stream + partial[0, 0].astype(F32)
    for distance, copy in enumerate(copies):
        copy.wait_recv()
        total += summed[0, distance + 1].astype(F32)
    stream = total.astype(BF16).astype(F32)

    gathered[1, 0] = norm_rows(stream, gain[1:2, :], bias[1:2, :])
    copies = exchange(gathered.at[1], gathered.at[1], 2, True)
    for copy in copies:
        copy.wait_recv()
    tokens = gathered[1].reshape(256, -1)
    units = wdown.shape[0] * wdown.shape[1]
    sums = dot(tokens, wgv[...].reshape(2 * units, -1), 1, 1)
    gate, value = sums[:, :units], sums[:, units:]
    hidden[...] = (value * (gate * (lax.erf(gate * (0.5**0.5)) + 1.0) * 0.5)).astype(BF16)
    terms = dot(hidden[...], wdown[...].reshape(units, -1), 1, 0)
    partial[1] = terms.astype(BF16).reshape(partial.shape[1:])
    copies = exchange(partial.at[1], summed.at[1], 3, False)
    total = stream + partial[1, 0].astype(F32)
    for distance, copy in enumerate(copies):
        copy.wait_recv()
        total += summed[1, distance + 1].astype(F32)
    result[...] = total.astype(BF16)

    for copy in started:
        copy.wait_send()
    send_foreign.wait_send()

    @pl.when(jj >= 1)
    def _():
        send_outward(jj, sem_ps.at[2]).wait_send()

    @pl.when(jj <= 2)
    def _():
        send_inward(jj, sem_ps.at[3]).wait_send()

    lax.fori_loop(0, 8, finish_step, 0)


def per_device(latent, ln_gain, ln_bias, w_qkv, w_out, w_gate, w_value, w_down):
    width = latent.shape[-1]
    own_rows = w_gate.shape[2]
    vmem, anywhere = pl.BlockSpec(memory_space=pltpu.VMEM), pl.BlockSpec(memory_space=pl.ANY)
    dma = pltpu.SemaphoreType.DMA
    stream = pl.pallas_call(
        block_kernel,
        out_shape=jax.ShapeDtypeStruct((32, width), BF16),
        in_specs=[vmem] * 3 + [anywhere] * 5,
        out_specs=vmem,
        scratch_shapes=[
            pltpu.VMEM((2, 8, 32, width), BF16),
            pltpu.VMEM((2, 8, 32, width), BF16),
            pltpu.VMEM((2, 8, 32, width), BF16),
            pltpu.VMEM((8, 2, 256, 2 * HD), BF16),
            pltpu.VMEM((256, 2 * HD), BF16),
            pltpu.VMEM((2 * HD, 512), BF16),
            pltpu.VMEM((2, 2 * HD, width), BF16),
            pltpu.VMEM((2, HD, width), BF16),
            pltpu.VMEM((2, HD, width), BF16),
            pltpu.VMEM((4, own_rows, width), BF16),
            pltpu.VMEM((2, own_rows, width), BF16),
            pltpu.VMEM((1, 512), F32),
            pltpu.VMEM((2 * HD, 512), F32),
            pltpu.VMEM((2 * HD, 256), BF16),
            pltpu.VMEM((HD, 256), BF16),
            pltpu.VMEM((HD, 256), BF16),
            pltpu.VMEM((256, 2 * own_rows), BF16),
            dma((6,)),
            dma((6,)),
            dma((6,)),
            dma((4, 8)),
            dma((4, 8)),
            dma((8,)),
            dma((8,)),
            dma((8,)),
            dma((8,)),
            dma((2,)),
            dma((5,)),
        ],
        compiler_params=pltpu.CompilerParams(
            collective_id=0, has_side_effects=True, vmem_limit_bytes=56 * 2**20
        ),
        name="transformer_block",
    )(
        latent.reshape(32, width),
        ln_gain[0],
        ln_bias[0],
        w_qkv[0].transpose(1, 0, 2).reshape(3 * HD, width),
        w_out[0],
        w_gate[0].T,
        w_value[0].T,
        w_down[0],
    )
    return stream.reshape(latent.shape)


def solution(mesh):
    return jax.shard_map(
        per_device,
        mesh=mesh,
        in_specs=(
            P("rows", "cols", None),
            P(),
            P(),
            P(None, "cols", None, None),
            P(None, "cols", None),
            P(None, None, "cols"),
            P(None, None, "cols"),
            P(None, "cols", None),
        ),
        out_specs=P("rows", "cols", None),
        check_vma=False,
    )
```

```python
import math

import jax
import jax.numpy as jnp
from jax import lax
from jax.experimental import pallas as pl
from jax.experimental.pallas import tpu as pltpu
from jax.sharding import PartitionSpec as P

HD = 64
MESH = pl.DeviceIdType.MESH
F32, BF16 = jnp.float32, jnp.bfloat16


def norm_rows(values, gain, bias):
    row_mean = jnp.mean(values, axis=-1, keepdims=True)
    centred = values - row_mean
    row_var = jnp.mean(centred * centred, axis=-1, keepdims=True)
    return (centred * lax.rsqrt(row_var + 1e-05) * gain + bias).astype(BF16)


def dot(left, right, left_dim, right_dim):
    return lax.dot_general(
        left, right, (((left_dim,), (right_dim,)), ((), ())), preferred_element_type=F32
    )


def block_kernel(
    latent, gain, bias, w_qkv, w_out, w_gate, w_value, w_down, result,
    rows_in, tokens, stream, partial, summed, keys, other_keys, query, query_other,
    wkv, wq, wo, wgv, wdown, top, accum, attended, attended_other,
    sem_w, sem_ws, sem_wr, sem_os, sem_or, sem_fs, sem_fr, sem_xs, sem_xr,
    sem_as, sem_ar, sem_zs, sem_zr, sem_gs, sem_cs, sem_cr, sem_ps, sem_pr,
):
    row, col = lax.axis_index("rows"), lax.axis_index("cols")
    core, me = col % 2, col // 2
    mate = lax.bitwise_xor(core, row % 8 // 4)
    sibling = (row, col + 1 - 2 * core)

    def chip(distance):
        return (row, lax.bitwise_xor(col, 2 * distance))

    def plane(distance):
        return (lax.bitwise_xor(row, distance), col)

    def remote(src, dst, send, recv, device):
        return pltpu.make_async_remote_copy(
            src_ref=src, dst_ref=dst, send_sem=send, recv_sem=recv, device_id=device, device_id_type=MESH
        )

    started = []

    def begin(*args):
        copy = remote(*args)
        copy.start()
        started.append(copy)
        return copy

    barrier = pltpu.get_barrier_semaphore()
    for distance in range(1, 8):
        pl.semaphore_signal(barrier, inc=1, device_id=chip(distance), device_id_type=MESH)
    for distance in range(1, 5):
        pl.semaphore_signal(barrier, inc=1, device_id=plane(distance), device_id_type=MESH)
    pl.semaphore_signal(barrier, inc=1, device_id=sibling, device_id_type=MESH)
    pl.semaphore_wait(barrier, 12)

    for distance in range(7, 0, -1):
        begin(latent, rows_in.at[me], sem_xs.at[distance], sem_xr.at[distance], chip(distance))
    rows_in[me] = latent[...]
    weights = []

    def load_weight(index, src, mine, theirs):
        own = pltpu.make_async_copy(src, mine, sem_w.at[index])
        own.start()
        weights.append((own, begin(src, theirs, sem_ws.at[index], sem_wr.at[index], sibling)))

    load_weight(0, w_qkv.at[pl.ds(HD, 2 * HD)], wkv.at[mate], wkv.at[mate])
    load_weight(1, w_qkv.at[pl.ds(0, HD)], wq.at[mate], wq.at[mate])
    load_weight(2, w_out, wo.at[0, mate], wo.at[0, mate])
    load_weight(3, w_gate, wgv.at[0], wgv.at[1])
    load_weight(4, w_value, wgv.at[2], wgv.at[3])
    load_weight(5, w_down, wdown.at[0], wdown.at[1])

    def rows_copy(distance):
        return remote(
            latent, rows_in.at[lax.bitwise_xor(me, distance)], sem_xs.at[distance], sem_xr.at[distance], chip(distance)
        )

    def first_norm(index, carry):
        slot = lax.bitwise_xor(me, index)

        @pl.when(index >= 1)
        def _():
            rows_copy(index).wait_recv()

        tokens[slot] = norm_rows(rows_in[slot].astype(F32), gain[0:1, :], bias[0:1, :])
        return carry

    lax.fori_loop(0, 8, first_norm, 0)
    for own, sent in weights[:2]:
        own.wait()
        sent.wait_recv()

    every = tokens[...].reshape(256, -1)
    packed = dot(every, wkv[...].reshape(4 * HD, -1), 1, 1).astype(BF16)
    other_keys[...] = packed[:, 2 * HD :]
    begin(other_keys, keys.at[4, core], sem_zs.at[4], sem_zr.at[4], plane(4))
    scale = HD ** (-0.5) * math.log2(math.e)
    queries = (dot(wq[...].reshape(2 * HD, -1), every, 1, 1) * scale).astype(BF16)
    query_other[...] = queries[HD:]
    send_query = begin(
        query_other, query.at[pl.ds(0, HD), pl.ds(256, 256)], sem_ps.at[0], sem_pr.at[0], plane(4)
    )
    keys[0, core] = packed[:, : 2 * HD]
    for distance in range(1, 4):
        begin(
            keys.at[0, core], keys.at[distance, core], sem_zs.at[distance], sem_zr.at[distance], plane(distance)
        )

    def send_sibling(slot):
        block = keys.at[slot, core]
        return remote(block, block, sem_gs.at[slot], sem_cr.at[slot], sibling)

    def from_sibling(slot):
        block = keys.at[slot, 1 - core]
        return remote(block, block, sem_gs.at[slot], sem_cr.at[slot], sibling)

    def from_plane(slot):
        block = keys.at[slot, core]
        return remote(block, block, sem_zs.at[slot], sem_zr.at[slot], plane(4))

    def spread(distance):
        return remote(
            keys.at[4, core], keys.at[4 + distance, core], sem_zs.at[4 + distance], sem_zr.at[4 + distance], plane(distance)
        )

    send_sibling(0).start()
    copies_out = [
        begin(w_out, wo.at[distance, mate], sem_os.at[distance], sem_or.at[distance], chip(distance))
        for distance in range(7, 0, -1)
    ]
    query[0:HD, 0:256] = queries[:HD]
    query[HD:, :] = jnp.zeros((HD, 512), BF16)
    top[...] = jnp.full(top.shape, -1e30, F32)
    accum[...] = jnp.zeros(accum.shape, F32)
    ones_lane = lax.broadcasted_iota(jnp.int32, (256, 2 * HD), 1) < HD
    send_query.wait_recv()

    def fold(index, carry):
        slot = index // 8 * 4 + index % 4
        second = index // 4 % 2
        which = core + second - 2 * core * second

        @pl.when(jnp.logical_and(second == 0, slot >= 1))
        def _():
            from_plane(slot).wait_recv()
            send_sibling(slot).start()

        @pl.when(index == 8)
        def _():
            for distance in range(1, 4):
                spread(distance).start()

        @pl.when(second == 1)
        def _():
            from_sibling(slot).wait_recv()

        block = keys[slot, which]
        scores = dot(block, query[...], 1, 0)
        old = top[...]
        new = jnp.maximum(old, jnp.max(scores, axis=0, keepdims=True))
        probs = jnp.exp2(scores - new).astype(BF16)
        values = jnp.where(ones_lane, jnp.ones_like(block), block)
        accum[...] = accum[...] * jnp.exp2(old - new) + dot(values, probs, 0, 0)
        top[...] = new
        return carry

    lax.fori_loop(0, 16, fold, 0)

    final = (accum[HD:, :] / accum[0:1, :]).astype(BF16)
    attended_other[...] = final[:, 256:]
    returned = begin(
        attended_other, attended.at[0, pl.ds(HD, HD)], sem_ps.at[1], sem_pr.at[1], plane(4)
    )
    attended[0, 0:HD] = final[:, :256]
    copies = []
    for distance in range(7, 0, -1):
        copies.append(
            begin(
                attended.at[0, pl.ds(0, HD)], attended.at[distance, pl.ds(0, HD)],
                sem_as.at[0, distance], sem_ar.at[0, distance], chip(distance),
            )
        )
    weights[2][0].wait()
    weights[2][1].wait_recv()
    forwarded = []
    for copy, distance in zip(copies_out, range(7, 0, -1)):
        copy.wait_recv()
        begin(wo.at[distance, mate], wo.at[distance, mate], sem_fs.at[distance], sem_fr.at[distance], sibling)
        theirs = wo.at[distance, 1 - mate]
        forwarded.append(remote(theirs, theirs, sem_fs.at[distance], sem_fr.at[distance], sibling))
    returned.wait_recv()
    for distance in range(7, 0, -1):
        copies.append(
            begin(
                attended.at[0, pl.ds(HD, HD)], attended.at[distance, pl.ds(HD, HD)],
                sem_as.at[1, distance], sem_ar.at[1, distance], chip(distance),
            )
        )
    for copy in forwarded:
        copy.wait_recv()
    for own, sent in weights[3:]:
        own.wait()
        sent.wait_recv()
    for copy in copies:
        copy.wait_recv()
    attn_sum = dot(attended[...].reshape(16 * HD, 256), wo[...].reshape(16 * HD, -1), 0, 0)
    stream[...] = (rows_in[...].reshape(256, -1).astype(F32) + attn_sum).astype(BF16).reshape(stream.shape)

    units = wdown.shape[0] * wdown.shape[1]

    def piece(slot):
        return remote(
            partial.at[lax.bitwise_xor(me, slot)], summed.at[slot], sem_cs.at[0, slot], sem_cs.at[1, slot], chip(slot)
        )

    def feed(index, carry):
        base = 4 * lax.bitwise_xor(1 - index, me // 4)
        rows = stream[pl.ds(base, 4)].reshape(128, -1).astype(F32)
        normed = norm_rows(rows, gain[1:2, :], bias[1:2, :])
        sums = dot(normed, wgv[...].reshape(2 * units, -1), 1, 1)
        gate, value = sums[:, :units], sums[:, units:]
        hidden = (value * (gate * (lax.erf(gate * (0.5**0.5)) + 1.0) * 0.5)).astype(BF16)
        terms = dot(hidden, wdown[...].reshape(units, -1), 1, 0)
        partial[pl.ds(base, 4)] = terms.astype(BF16).reshape(4, 32, -1)
        for offset in range(3, -1, -1):
            distance = 4 - 4 * index + offset

            @pl.when(distance >= 1)
            def _():
                piece(distance).start()

        return carry

    lax.fori_loop(0, 2, feed, 0)
    total = stream[me].astype(F32) + partial[me].astype(F32)
    for distance in range(1, 8):
        piece(distance).wait_recv()
        total += summed[distance].astype(F32)
    result[...] = total.astype(BF16)

    for copy in started:
        copy.wait_send()
    for distance in range(1, 4):
        spread(distance).wait_send()

    def finish(slot, carry):
        send_sibling(slot).wait_send()

        @pl.when(slot >= 1)
        def _():
            piece(slot).wait_send()

        return carry

    lax.fori_loop(0, 8, finish, 0)


def per_device(latent, ln_gain, ln_bias, w_qkv, w_out, w_gate, w_value, w_down):
    width = latent.shape[-1]
    own_units = w_gate.shape[2]
    vmem, anywhere = pl.BlockSpec(memory_space=pltpu.VMEM), pl.BlockSpec(memory_space=pl.ANY)
    dma = pltpu.SemaphoreType.DMA
    stream = pl.pallas_call(
        block_kernel,
        out_shape=jax.ShapeDtypeStruct((32, width), BF16),
        in_specs=[vmem] * 3 + [anywhere] * 5,
        out_specs=vmem,
        scratch_shapes=[
            pltpu.VMEM((8, 32, width), BF16),
            pltpu.VMEM((8, 32, width), BF16),
            pltpu.VMEM((8, 32, width), BF16),
            pltpu.VMEM((8, 32, width), BF16),
            pltpu.VMEM((8, 32, width), BF16),
            pltpu.VMEM((8, 2, 256, 2 * HD), BF16),
            pltpu.VMEM((256, 2 * HD), BF16),
            pltpu.VMEM((2 * HD, 512), BF16),
            pltpu.VMEM((HD, 256), BF16),
            pltpu.VMEM((2, 2 * HD, width), BF16),
            pltpu.VMEM((2, HD, width), BF16),
            pltpu.VMEM((8, 2, HD, width), BF16),
            pltpu.VMEM((4, own_units, width), BF16),
            pltpu.VMEM((2, own_units, width), BF16),
            pltpu.VMEM((1, 512), F32),
            pltpu.VMEM((2 * HD, 512), F32),
            pltpu.VMEM((8, 2 * HD, 256), BF16),
            pltpu.VMEM((HD, 256), BF16),
            dma((6,)),
            dma((6,)),
            dma((6,)),
            dma((8,)),
            dma((8,)),
            dma((8,)),
            dma((8,)),
            dma((8,)),
            dma((8,)),
            dma((2, 8)),
            dma((2, 8)),
            dma((8,)),
            dma((8,)),
            dma((8,)),
            dma((2, 8)),
            dma((8,)),
            dma((2,)),
            dma((2,)),
        ],
        compiler_params=pltpu.CompilerParams(
            collective_id=0, has_side_effects=True, vmem_limit_bytes=56 * 2**20
        ),
        name="transformer_block",
    )(
        latent.reshape(32, width),
        ln_gain[0],
        ln_bias[0],
        w_qkv[0].transpose(1, 0, 2).reshape(3 * HD, width),
        w_out[0],
        w_gate[0].T,
        w_value[0].T,
        w_down[0],
    )
    return stream.reshape(latent.shape)


def solution(mesh):
    return jax.shard_map(
        per_device,
        mesh=mesh,
        in_specs=(
            P("rows", "cols", None),
            P(),
            P(),
            P(None, "cols", None, None),
            P(None, "cols", None),
            P(None, None, "cols"),
            P(None, None, "cols"),
            P(None, "cols", None),
        ),
        out_specs=P("rows", "cols", None),
        check_vma=False,
    )
```

```python
import math

import jax
import jax.numpy as jnp
from jax import lax
from jax.experimental import pallas as pl
from jax.experimental.pallas import tpu as pltpu
from jax.sharding import PartitionSpec as P

HD = 64
MESH = pl.DeviceIdType.MESH
F32, BF16 = jnp.float32, jnp.bfloat16


def norm_rows(values, gain, bias):
    row_mean = jnp.mean(values, axis=-1, keepdims=True)
    centred = values - row_mean
    row_var = jnp.mean(centred * centred, axis=-1, keepdims=True)
    return (centred * lax.rsqrt(row_var + 1e-05) * gain + bias).astype(BF16)


def dot(left, right, left_dim, right_dim):
    return lax.dot_general(
        left, right, (((left_dim,), (right_dim,)), ((), ())), preferred_element_type=F32
    )


def block_kernel(
    latent, gain_in, bias_in, w_qkv, w_out, w_gate, w_value, w_down, result,
    rows_in, rows_far, gain, bias, tokens, stream, partial, summed, keys, query,
    wkv, wq, wo, wgv, wdown, top, accum, attended, attended_other,
    sem_l, sem_w, sem_ws, sem_wr, sem_os, sem_or, sem_fs, sem_fr, sem_xs, sem_xr, sem_ys, sem_yr,
    sem_as, sem_ar, sem_zs, sem_zr, sem_gs, sem_gr, sem_cs, sem_cr, sem_ps, sem_pr,
):
    row, col = lax.axis_index("rows"), lax.axis_index("cols")
    core, me = col % 2, col // 2
    mate = lax.bitwise_xor(core, row % 8 // 4)
    sibling = (row, col + 1 - 2 * core)
    width = gain.shape[1]

    def chip(distance):
        return (row, lax.bitwise_xor(col, 2 * distance))

    def plane(distance):
        return (lax.bitwise_xor(row, distance), col)

    def remote(src, dst, send, recv, device):
        return pltpu.make_async_remote_copy(
            src_ref=src, dst_ref=dst, send_sem=send, recv_sem=recv, device_id=device, device_id_type=MESH
        )

    started = []

    def begin(*args):
        copy = remote(*args)
        copy.start()
        started.append(copy)
        return copy

    barrier = pltpu.get_barrier_semaphore()
    pl.semaphore_signal(barrier, inc=1, device_id=plane(4), device_id_type=MESH)
    for distance in range(7, 0, -1):
        pl.semaphore_signal(barrier, inc=1, device_id=chip(distance), device_id_type=MESH)
    for distance in range(1, 4):
        pl.semaphore_signal(barrier, inc=1, device_id=plane(distance), device_id_type=MESH)
    pl.semaphore_signal(barrier, inc=1, device_id=sibling, device_id_type=MESH)

    local = []

    def begin_local(src, dst, sem):
        copy = pltpu.make_async_copy(src, dst, sem)
        copy.start()
        return copy

    local = [
        begin_local(latent, rows_in.at[me], sem_l.at[0]),
        begin_local(gain_in, gain, sem_l.at[1]),
        begin_local(bias_in, bias, sem_l.at[2]),
    ]
    homes = [
        (w_qkv.at[pl.ds(HD, 2 * HD)], wkv.at[mate], wkv.at[mate]),
        (w_qkv.at[pl.ds(0, HD)], wq.at[mate], wq.at[mate]),
        (w_out, wo.at[0, mate], wo.at[0, mate]),
        (w_gate, wgv.at[0], wgv.at[1]),
        (w_value, wgv.at[2], wgv.at[3]),
        (w_down, wdown.at[0], wdown.at[1]),
    ]
    own_weights = [begin_local(src, mine, sem_w.at[index]) for index, (src, mine, _) in enumerate(homes)]
    pl.semaphore_wait(barrier, 12)

    across = begin(latent, rows_far.at[me], sem_ps.at[0], sem_pr.at[0], plane(4))
    for distance in range(7, 0, -1):
        begin(latent, rows_in.at[me], sem_xs.at[distance], sem_xr.at[distance], chip(distance))
    sent_weights = [
        begin(src, theirs, sem_ws.at[index], sem_wr.at[index], sibling)
        for index, (src, _, theirs) in enumerate(homes)
    ]

    def near_copy(distance):
        block = rows_in.at[lax.bitwise_xor(me, distance)]
        return remote(block, block, sem_xs.at[distance], sem_xr.at[distance], chip(distance))

    def far_copy(distance):
        block = rows_far.at[lax.bitwise_xor(me, distance)]
        return remote(block, block, sem_ys.at[distance], sem_yr.at[distance], chip(distance))

    def near_norm(distance):
        slot = lax.bitwise_xor(me, distance)
        rows = rows_in[slot].astype(F32).reshape(32, width)
        stream[slot] = rows.astype(BF16)
        tokens[0, slot] = norm_rows(rows, gain[0:1, :], bias[0:1, :])

    def near_step(distance, carry):
        near_copy(distance).wait_recv()
        near_norm(distance)
        return carry

    for copy in local:
        copy.wait()
    near_norm(0)
    across.wait_recv()
    for distance in range(7, 0, -1):
        begin(rows_far.at[me], rows_far.at[me], sem_ys.at[distance], sem_yr.at[distance], chip(distance))
    lax.fori_loop(1, 8, near_step, 0)
    for index in range(2):
        own_weights[index].wait()
        sent_weights[index].wait_recv()

    scale = HD ** (-0.5) * math.log2(math.e)

    def project(which, slot, part):
        piece = tokens[which, pl.ds(4 * part, 4)].reshape(128, width)
        place = pl.ds(pl.multiple_of(128 * part, 128), 128)
        keys[slot, core, place] = dot(piece, wkv[0], 1, 1).astype(BF16)
        query[which, 0:HD, place] = (dot(wq[0], piece, 1, 1) * scale).astype(BF16)

    def send_sibling(slot):
        block = keys.at[slot, core]
        return remote(block, block, sem_gs.at[slot], sem_gr.at[slot], sibling)

    def from_sibling(slot):
        block = keys.at[slot, 1 - core]
        return remote(block, block, sem_gs.at[slot], sem_gr.at[slot], sibling)

    def from_plane(slot, part):
        block = keys.at[slot, core, pl.ds(128 * part, 128)]
        return remote(block, block, sem_zs.at[slot, part], sem_zr.at[slot, part], plane(4))

    for part in range(2):
        project(0, 0, part)
    for distance in range(3, 0, -1):
        begin(
            keys.at[0, core], keys.at[distance, core],
            sem_zs.at[distance, 0], sem_zr.at[distance, 0], plane(distance),
        )
    send_sibling(0).start()
    query[:, HD:, :] = jnp.zeros((2, HD, 256), BF16)
    top[...] = jnp.full(top.shape, -1e30, F32)
    accum[...] = jnp.zeros(accum.shape, F32)
    ones_lane = lax.broadcasted_iota(jnp.int32, (512, 2 * HD), 1) < HD

    def fold(slot, which):
        block = keys[slot].reshape(512, 2 * HD)
        scores = dot(block, query[which], 1, 0)
        old = top[which]
        new = jnp.maximum(old, jnp.max(scores, axis=0, keepdims=True))
        probs = jnp.exp2(scores - new).astype(BF16)
        values = jnp.where(ones_lane, jnp.ones_like(block), block)
        accum[which] = accum[which] * jnp.exp2(old - new) + dot(values, probs, 0, 0)
        top[which] = new

    def attended_by(which):
        return (accum[which, HD:, :] / accum[which, 0:1, :]).astype(BF16)

    from_sibling(0).wait_recv()
    fold(0, 0)

    def far_step(distance, carry):
        @pl.when(distance >= 1)
        def _():
            far_copy(distance).wait_recv()

        slot = lax.bitwise_xor(me, distance)
        rows = rows_far[slot].astype(F32).reshape(32, width)
        tokens[1, slot] = norm_rows(rows, gain[0:1, :], bias[0:1, :])
        return carry

    for turn in range(2):
        part = lax.bitwise_xor(me // 4, turn)
        lax.fori_loop(4 * turn, 4 * turn + 4, far_step, 0)
        project(1, 4, part)
        place = pl.ds(pl.multiple_of(128 * part, 128), 128)
        for distance in range(3, 0, -1):
            begin(
                keys.at[4, core, place], keys.at[4 + distance, core, place],
                sem_zs.at[4 + distance, turn], sem_zr.at[4 + distance, turn], plane(distance),
            )
    send_sibling(4).start()
    copies_out = [
        begin(w_out, wo.at[distance, mate], sem_os.at[distance], sem_or.at[distance], chip(distance))
        for distance in range(7, 0, -1)
    ]

    def early(index, carry):
        slots, halves = carry
        slot, which = slots % 8, halves % 2

        @pl.when(index == 1)
        def _():
            for near in range(1, 4):
                block = keys.at[near, core]
                remote(block, block, sem_zs.at[near, 0], sem_zr.at[near, 0], plane(near)).wait_recv()
                send_sibling(near).start()

        @pl.when(jnp.logical_or(index == 1, jnp.logical_and(index >= 3, index < 6)))
        def _():
            from_sibling(slot).wait_recv()

        @pl.when(index == 6)
        def _():
            for far in range(5, 8):
                from_plane(far, 0).wait_recv()
                from_plane(far, 1).wait_recv()
                send_sibling(far).start()

        fold(slot, which)
        return (slots // 8, halves // 2)

    order = sum(slot * 8**place for place, slot in enumerate((0, 4, 4, 1, 2, 3, 1, 2, 3)))
    halves = sum(half * 2**place for place, half in enumerate((1, 1, 0, 1, 1, 1, 0, 0, 0)))
    lax.fori_loop(0, 9, early, (jnp.int32(order), jnp.int32(halves)))

    returned = remote(
        attended_other, attended.at[0, pl.ds(HD, HD)], sem_ps.at[1], sem_pr.at[1], plane(4)
    )

    def late(index, carry):
        slot, which = 5 + index % 3, 1 - index // 3

        @pl.when(index < 3)
        def _():
            from_sibling(slot).wait_recv()

        @pl.when(index == 3)
        def _():
            attended_other[...] = attended_by(1)
            returned.start()

        fold(slot, which)
        return carry

    lax.fori_loop(0, 6, late, 0)

    attended[0, 0:HD] = attended_by(0)
    copies = []
    for distance in range(7, 0, -1):
        copies.append(
            begin(
                attended.at[0, pl.ds(0, HD)], attended.at[distance, pl.ds(0, HD)],
                sem_as.at[0, distance], sem_ar.at[0, distance], chip(distance),
            )
        )
    for index in range(2, 6):
        own_weights[index].wait()
        sent_weights[index].wait_recv()
    returned.wait_recv()
    for distance in range(7, 0, -1):
        copies.append(
            begin(
                attended.at[0, pl.ds(HD, HD)], attended.at[distance, pl.ds(HD, HD)],
                sem_as.at[1, distance], sem_ar.at[1, distance], chip(distance),
            )
        )
    forwarded = []
    for copy, distance in zip(copies_out, range(7, 0, -1)):
        copy.wait_recv()
        begin(wo.at[distance, mate], wo.at[distance, mate], sem_fs.at[distance], sem_fr.at[distance], sibling)
        theirs = wo.at[distance, 1 - mate]
        forwarded.append(remote(theirs, theirs, sem_fs.at[distance], sem_fr.at[distance], sibling))
    for copy in forwarded:
        copy.wait_recv()
    for copy in copies:
        copy.wait_recv()
    attn_sum = dot(attended[...].reshape(16 * HD, 256), wo[...].reshape(16 * HD, width), 0, 0)
    stream[...] = (stream[...].reshape(256, width).astype(F32) + attn_sum).astype(BF16).reshape(stream.shape)

    units = wdown.shape[0] * wdown.shape[1]

    def piece(slot):
        return remote(
            partial.at[lax.bitwise_xor(me, slot)], summed.at[slot], sem_cs.at[slot], sem_cr.at[slot], chip(slot)
        )

    def feed(index, carry):
        base = 4 * lax.bitwise_xor(1 - index, me // 4)
        rows = stream[pl.ds(base, 4)].reshape(128, width).astype(F32)
        normed = norm_rows(rows, gain[1:2, :], bias[1:2, :])
        sums = dot(normed, wgv[...].reshape(2 * units, width), 1, 1)
        gate, value = sums[:, :units], sums[:, units:]
        hidden = (value * (gate * (lax.erf(gate * (0.5**0.5)) + 1.0) * 0.5)).astype(BF16)
        terms = dot(hidden, wdown[...].reshape(units, width), 1, 0)
        partial[pl.ds(base, 4)] = terms.astype(BF16).reshape(4, 32, width)
        for offset in range(3, -1, -1):
            distance = 4 - 4 * index + offset

            @pl.when(distance >= 1)
            def _():
                piece(distance).start()

        return carry

    lax.fori_loop(0, 2, feed, 0)
    total = stream[me].astype(F32) + partial[me].astype(F32)
    for distance in range(1, 8):
        piece(distance).wait_recv()
        total += summed[distance].astype(F32)
    result[...] = total.reshape(8, 4, width).astype(BF16)

    for copy in started:
        copy.wait_send()
    returned.wait_send()

    def finish(slot, carry):
        send_sibling(slot).wait_send()

        @pl.when(slot >= 1)
        def _():
            piece(slot).wait_send()

        return carry

    lax.fori_loop(0, 8, finish, 0)


def per_device(latent, ln_gain, ln_bias, w_qkv, w_out, w_gate, w_value, w_down):
    width = latent.shape[-1]
    own_units = w_gate.shape[2]
    vmem, anywhere = pl.BlockSpec(memory_space=pltpu.VMEM), pl.BlockSpec(memory_space=pl.ANY)
    dma = pltpu.SemaphoreType.DMA
    return pl.pallas_call(
        block_kernel,
        out_shape=jax.ShapeDtypeStruct(latent.shape, BF16),
        in_specs=[anywhere] * 8,
        out_specs=vmem,
        scratch_shapes=[
            pltpu.VMEM((8, *latent.shape), BF16),
            pltpu.VMEM((8, *latent.shape), BF16),
            pltpu.VMEM((2, width), F32),
            pltpu.VMEM((2, width), F32),
            pltpu.VMEM((2, 8, 32, width), BF16),
            pltpu.VMEM((8, 32, width), BF16),
            pltpu.VMEM((8, 32, width), BF16),
            pltpu.VMEM((8, 32, width), BF16),
            pltpu.VMEM((8, 2, 256, 2 * HD), BF16),
            pltpu.VMEM((2, 2 * HD, 256), BF16),
            pltpu.VMEM((2, 2 * HD, width), BF16),
            pltpu.VMEM((2, HD, width), BF16),
            pltpu.VMEM((8, 2, HD, width), BF16),
            pltpu.VMEM((4, own_units, width), BF16),
            pltpu.VMEM((2, own_units, width), BF16),
            pltpu.VMEM((2, 1, 256), F32),
            pltpu.VMEM((2, 2 * HD, 256), F32),
            pltpu.VMEM((8, 2 * HD, 256), BF16),
            pltpu.VMEM((HD, 256), BF16),
            dma((3,)),
            dma((6,)),
            dma((6,)),
            dma((6,)),
            dma((8,)),
            dma((8,)),
            dma((8,)),
            dma((8,)),
            dma((8,)),
            dma((8,)),
            dma((8,)),
            dma((8,)),
            dma((2, 8)),
            dma((2, 8)),
            dma((8, 2)),
            dma((8, 2)),
            dma((8,)),
            dma((8,)),
            dma((8,)),
            dma((8,)),
            dma((2,)),
            dma((2,)),
        ],
        compiler_params=pltpu.CompilerParams(
            collective_id=0, has_side_effects=True, vmem_limit_bytes=56 * 2**20
        ),
        name="transformer_block",
    )(
        latent,
        ln_gain[0],
        ln_bias[0],
        w_qkv[0].transpose(1, 0, 2).reshape(3 * HD, width),
        w_out[0],
        w_gate[0].T,
        w_value[0].T,
        w_down[0],
    )


def solution(mesh):
    return jax.shard_map(
        per_device,
        mesh=mesh,
        in_specs=(
            P("rows", "cols", None),
            P(),
            P(),
            P(None, "cols", None, None),
            P(None, "cols", None),
            P(None, None, "cols"),
            P(None, None, "cols"),
            P(None, "cols", None),
        ),
        out_specs=P("rows", "cols", None),
        check_vma=False,
    )
```

```python
import math

import jax
import jax.numpy as jnp
from jax import lax
from jax.experimental import pallas as pl
from jax.experimental.pallas import tpu as pltpu
from jax.sharding import PartitionSpec as P

HD = 64
MESH = pl.DeviceIdType.MESH
F32, BF16 = jnp.float32, jnp.bfloat16


def norm_rows(values, gain, bias):
    row_mean = jnp.mean(values, axis=-1, keepdims=True)
    centred = values - row_mean
    row_var = jnp.mean(centred * centred, axis=-1, keepdims=True)
    return (centred * lax.rsqrt(row_var + 1e-05) * gain + bias).astype(BF16)


def dot(left, right, left_dim, right_dim):
    return lax.dot_general(
        left, right, (((left_dim,), (right_dim,)), ((), ())), preferred_element_type=F32
    )


def block_kernel(
    latent, gain_in, bias_in, w_qkv, w_out, w_gate, w_value, w_down, result,
    rows_in, rows_far, gain, bias, tokens, stream, partial, summed, keys, query,
    wkv, wq, wo, wgv, wgv_t, wdown, top, accum, attn_sum, attended, attended_other,
    sem_l, sem_w, sem_ws, sem_wr, sem_os, sem_or, sem_fs, sem_fr, sem_xs, sem_xr, sem_ys, sem_yr,
    sem_as, sem_ar, sem_zs, sem_zr, sem_gs, sem_gr, sem_cs, sem_cr, sem_ps, sem_pr,
):
    row, col = lax.axis_index("rows"), lax.axis_index("cols")
    core, me = col % 2, col // 2
    mate = lax.bitwise_xor(core, row % 8 // 4)
    sibling = (row, col + 1 - 2 * core)
    width = gain.shape[1]

    def chip(distance):
        return (row, lax.bitwise_xor(col, 2 * distance))

    def plane(distance):
        return (lax.bitwise_xor(row, distance), col)

    def remote(src, dst, send, recv, device):
        return pltpu.make_async_remote_copy(
            src_ref=src, dst_ref=dst, send_sem=send, recv_sem=recv, device_id=device, device_id_type=MESH
        )

    started = []

    def begin(*args):
        copy = remote(*args)
        copy.start()
        started.append(copy)
        return copy

    barrier = pltpu.get_barrier_semaphore()
    pl.semaphore_signal(barrier, inc=1, device_id=plane(4), device_id_type=MESH)
    for distance in range(7, 0, -1):
        pl.semaphore_signal(barrier, inc=1, device_id=chip(distance), device_id_type=MESH)
    for distance in range(1, 4):
        pl.semaphore_signal(barrier, inc=1, device_id=plane(distance), device_id_type=MESH)
    pl.semaphore_signal(barrier, inc=1, device_id=sibling, device_id_type=MESH)

    local = []

    def begin_local(src, dst, sem):
        copy = pltpu.make_async_copy(src, dst, sem)
        copy.start()
        return copy

    local = [
        begin_local(latent, rows_in.at[me], sem_l.at[0]),
        begin_local(gain_in, gain, sem_l.at[1]),
        begin_local(bias_in, bias, sem_l.at[2]),
    ]
    homes = [
        (w_qkv.at[pl.ds(HD, 2 * HD)], wkv.at[mate], wkv.at[mate]),
        (w_qkv.at[pl.ds(0, HD)], wq.at[mate], wq.at[mate]),
        (w_out, wo.at[0, mate], wo.at[0, mate]),
        (w_gate, wgv.at[0], wgv.at[1]),
        (w_value, wgv.at[2], wgv.at[3]),
        (w_down, wdown.at[0], wdown.at[1]),
    ]

    def fetch(first, last):
        return [begin_local(homes[index][0], homes[index][1], sem_w.at[index]) for index in range(first, last)]

    def share(first, last):
        return [
            begin(homes[index][0], homes[index][2], sem_ws.at[index], sem_wr.at[index], sibling)
            for index in range(first, last)
        ]

    own_weights = fetch(0, 3)
    pl.semaphore_wait(barrier, 12)

    across = [
        begin(latent.at[pl.ds(4 * part, 4)], rows_far.at[me, part], sem_ps.at[part], sem_pr.at[part], plane(4))
        for part in range(2)
    ]
    for distance in range(7, 0, -1):
        begin(latent, rows_in.at[me], sem_xs.at[distance], sem_xr.at[distance], chip(distance))
    sent_weights = share(0, 3)

    def spread_out(part, first, count):
        return [
            begin(
                w_out.at[pl.ds(first, count)], wo.at[distance, mate, pl.ds(first, count)],
                sem_os.at[part, distance], sem_or.at[part, distance], chip(distance),
            )
            for distance in range(7, 0, -1)
        ]

    copies_out = spread_out(0, 0, 16)

    def near_copy(distance):
        block = rows_in.at[lax.bitwise_xor(me, distance)]
        return remote(block, block, sem_xs.at[distance], sem_xr.at[distance], chip(distance))

    def far_copy(part, distance):
        block = rows_far.at[lax.bitwise_xor(me, distance), part]
        return remote(block, block, sem_ys.at[part, distance], sem_yr.at[part, distance], chip(distance))

    def near_norm(distance):
        slot = lax.bitwise_xor(me, distance)
        for part in range(2):
            rows = rows_in[slot, pl.ds(4 * part, 4)].astype(F32).reshape(16, width)
            stream[part, slot] = rows.astype(BF16)
            tokens[0, part, slot] = norm_rows(rows, gain[0:1, :], bias[0:1, :])

    def near_step(distance, carry):
        near_copy(distance).wait_recv()
        near_norm(distance)
        return carry

    for copy in local:
        copy.wait()
    near_norm(0)
    for part in range(2):
        across[part].wait_recv()
        for distance in range(7, 0, -1):
            mine = rows_far.at[me, part]
            begin(mine, mine, sem_ys.at[part, distance], sem_yr.at[part, distance], chip(distance))
    own_weights += fetch(3, 6)
    sent_weights += share(3, 6)
    lax.fori_loop(1, 8, near_step, 0)
    for index in range(2):
        own_weights[index].wait()
        sent_weights[index].wait_recv()

    scale = HD ** (-0.5) * math.log2(math.e)

    def project(which, part):
        piece = tokens[which, part].reshape(128, width)
        place = pl.ds(128 * part, 128)
        keys[4 * which, core, place] = dot(piece, wkv[0], 1, 1).astype(BF16)
        query[0:HD, pl.ds(256 * which + 128 * part, 128)] = (dot(wq[0], piece, 1, 1) * scale).astype(BF16)

    def send_sibling(slot):
        block = keys.at[slot, core]
        return remote(block, block, sem_gs.at[slot], sem_gr.at[slot], sibling)

    def from_sibling(slot):
        block = keys.at[slot, 1 - core]
        return remote(block, block, sem_gs.at[slot], sem_gr.at[slot], sibling)

    def from_plane(slot, part):
        block = keys.at[slot, core, pl.ds(128 * part, 128)]
        return remote(block, block, sem_zs.at[slot, part], sem_zr.at[slot, part], plane(4))

    for part in range(2):
        project(0, part)
    for distance in range(3, 0, -1):
        begin(
            keys.at[0, core], keys.at[distance, core],
            sem_zs.at[distance, 0], sem_zr.at[distance, 0], plane(distance),
        )
    send_sibling(0).start()
    query[HD:, :] = jnp.zeros((HD, 512), BF16)
    own_weights[3].wait()
    own_weights[4].wait()
    sent_weights[3].wait_recv()
    sent_weights[4].wait_recv()
    for index in range(4):
        wgv_t[:, pl.ds(320 * index, 320)] = wgv[index].T

    def far_step(distance, part):
        @pl.when(distance >= 1)
        def _():
            far_copy(part, distance).wait_recv()

        slot = lax.bitwise_xor(me, distance)
        rows = rows_far[slot, part].astype(F32).reshape(16, width)
        tokens[1, part, slot] = norm_rows(rows, gain[0:1, :], bias[0:1, :])
        return part

    for part in range(2):
        lax.fori_loop(0, 8, far_step, part)
        project(1, part)
        place = pl.ds(128 * part, 128)
        for distance in range(3, 0, -1):
            begin(
                keys.at[4, core, place], keys.at[4 + distance, core, place],
                sem_zs.at[4 + distance, part], sem_zr.at[4 + distance, part], plane(distance),
            )
    send_sibling(4).start()
    copies_out += spread_out(1, 16, 48)

    def scored(block, first, count):
        return dot(block, query[:, first : first + count], 1, 0)

    def summed_values(block, probs):
        lanes = lax.broadcasted_iota(jnp.int32, block.shape, 1)
        return dot(jnp.where(lanes < HD, jnp.ones_like(block), block), probs, 0, 0)

    def fold(block, first, count):
        scores = scored(block, first, count)
        old = top[:, first : first + count]
        new = jnp.maximum(old, jnp.max(scores, axis=0, keepdims=True))
        probs = jnp.exp2(scores - new).astype(BF16)
        accum[:, first : first + count] = accum[:, first : first + count] * jnp.exp2(old - new) + summed_values(block, probs)
        top[:, first : first + count] = new

    def attended_by(first):
        return (accum[HD:, first : first + 256] / accum[0:1, first : first + 256]).astype(BF16)

    for near in range(1, 4):
        block = keys.at[near, core]
        remote(block, block, sem_zs.at[near, 0], sem_zr.at[near, 0], plane(near)).wait_recv()
        send_sibling(near).start()
    for near in range(4):
        from_sibling(near).wait_recv()
    block = keys[0:4].reshape(2048, 2 * HD)
    scores = scored(block, 0, 512)
    first_top = jnp.max(scores, axis=0, keepdims=True)
    top[...] = first_top
    accum[...] = summed_values(block, jnp.exp2(scores - first_top).astype(BF16))
    for far in range(5, 8):
        from_plane(far, 0).wait_recv()
        from_plane(far, 1).wait_recv()
        send_sibling(far).start()
    fold(keys[pl.ds(4, 4), core].reshape(1024, 2 * HD), 256, 256)
    for far in range(4, 8):
        from_sibling(far).wait_recv()
    fold(keys[pl.ds(4, 4), 1 - core].reshape(1024, 2 * HD), 256, 256)
    attended_other[...] = attended_by(256)
    returned = begin(
        attended_other, attended.at[0, pl.ds(HD, HD)], sem_ps.at[2], sem_pr.at[2], plane(4)
    )
    fold(keys[4:8].reshape(2048, 2 * HD), 0, 256)

    attended[0, 0:HD] = attended_by(0)
    copies = []
    for distance in range(7, 0, -1):
        copies.append(
            begin(
                attended.at[0, pl.ds(0, HD)], attended.at[distance, pl.ds(0, HD)],
                sem_as.at[0, distance], sem_ar.at[0, distance], chip(distance),
            )
        )
    returned.wait_recv()
    for distance in range(7, 0, -1):
        copies.append(
            begin(
                attended.at[0, pl.ds(HD, HD)], attended.at[distance, pl.ds(HD, HD)],
                sem_as.at[1, distance], sem_ar.at[1, distance], chip(distance),
            )
        )
    own_weights[2].wait()
    sent_weights[2].wait_recv()
    forwarded = []
    for index, distance in enumerate(range(7, 0, -1)):
        copies_out[index].wait_recv()
        copies_out[7 + index].wait_recv()
        begin(wo.at[distance, mate], wo.at[distance, mate], sem_fs.at[distance], sem_fr.at[distance], sibling)
        theirs = wo.at[distance, 1 - mate]
        forwarded.append(remote(theirs, theirs, sem_fs.at[distance], sem_fr.at[distance], sibling))
    for copy in forwarded + copies[:7]:
        copy.wait_recv()

    def projected(part):
        heads = attended[:, HD * part : HD * (part + 1)].reshape(8 * HD, 256)
        return dot(heads, wo[:, part].reshape(8 * HD, width), 0, 0)

    attn_sum[...] = projected(0)
    own_weights[5].wait()
    sent_weights[5].wait_recv()
    for copy in copies[7:]:
        copy.wait_recv()
    total = stream[...].reshape(256, width).astype(F32) + (attn_sum[...] + projected(1))
    stream[...] = total.astype(BF16).reshape(stream.shape)

    units = wdown.shape[0] * wdown.shape[1]

    def piece(slot):
        return remote(
            partial.at[:, lax.bitwise_xor(me, slot)], summed.at[slot], sem_cs.at[slot], sem_cr.at[slot], chip(slot)
        )

    def feed(index, carry):
        base = 4 * lax.bitwise_xor(1 - index, me // 4)
        rows = stream[:, pl.ds(base, 4)].reshape(128, width).astype(F32)
        normed = norm_rows(rows, gain[1:2, :], bias[1:2, :])
        sums = dot(normed, wgv_t[...], 1, 0)
        gate, value = sums[:, :units], sums[:, units:]
        hidden = (value * (gate * (lax.erf(gate * (0.5**0.5)) + 1.0) * 0.5)).astype(BF16)
        terms = dot(hidden, wdown[...].reshape(units, width), 1, 0)
        partial[:, pl.ds(base, 4)] = terms.astype(BF16).reshape(2, 4, 16, width)
        for offset in range(3, -1, -1):
            distance = 4 - 4 * index + offset

            @pl.when(distance >= 1)
            def _():
                piece(distance).start()

        return carry

    lax.fori_loop(0, 2, feed, 0)
    total = stream[:, me].astype(F32) + partial[:, me].astype(F32)
    for distance in range(1, 8):
        piece(distance).wait_recv()
        total += summed[distance].astype(F32)
    result[...] = total.reshape(8, 4, width).astype(BF16)

    for copy in started:
        copy.wait_send()

    def finish(slot, carry):
        send_sibling(slot).wait_send()

        @pl.when(slot >= 1)
        def _():
            piece(slot).wait_send()

        return carry

    lax.fori_loop(0, 8, finish, 0)


def per_device(latent, ln_gain, ln_bias, w_qkv, w_out, w_gate, w_value, w_down):
    width = latent.shape[-1]
    own_units = w_gate.shape[2]
    vmem, anywhere = pl.BlockSpec(memory_space=pltpu.VMEM), pl.BlockSpec(memory_space=pl.ANY)
    dma = pltpu.SemaphoreType.DMA
    return pl.pallas_call(
        block_kernel,
        out_shape=jax.ShapeDtypeStruct(latent.shape, BF16),
        in_specs=[anywhere] * 8,
        out_specs=vmem,
        scratch_shapes=[
            pltpu.VMEM((8, *latent.shape), BF16),
            pltpu.VMEM((8, 2, 4, *latent.shape[1:]), BF16),
            pltpu.VMEM((2, width), F32),
            pltpu.VMEM((2, width), F32),
            pltpu.VMEM((2, 2, 8, 16, width), BF16),
            pltpu.VMEM((2, 8, 16, width), BF16),
            pltpu.VMEM((2, 8, 16, width), BF16),
            pltpu.VMEM((8, 2, 16, width), BF16),
            pltpu.VMEM((8, 2, 256, 2 * HD), BF16),
            pltpu.VMEM((2 * HD, 512), BF16),
            pltpu.VMEM((2, 2 * HD, width), BF16),
            pltpu.VMEM((2, HD, width), BF16),
            pltpu.VMEM((8, 2, HD, width), BF16),
            pltpu.VMEM((4, own_units, width), BF16),
            pltpu.VMEM((width, 4 * own_units), BF16),
            pltpu.VMEM((2, own_units, width), BF16),
            pltpu.VMEM((1, 512), F32),
            pltpu.VMEM((2 * HD, 512), F32),
            pltpu.VMEM((256, width), F32),
            pltpu.VMEM((8, 2 * HD, 256), BF16),
            pltpu.VMEM((HD, 256), BF16),
            dma((3,)),
            dma((6,)),
            dma((6,)),
            dma((6,)),
            dma((2, 8)),
            dma((2, 8)),
            dma((8,)),
            dma((8,)),
            dma((8,)),
            dma((8,)),
            dma((2, 8)),
            dma((2, 8)),
            dma((2, 8)),
            dma((2, 8)),
            dma((8, 2)),
            dma((8, 2)),
            dma((8,)),
            dma((8,)),
            dma((8,)),
            dma((8,)),
            dma((3,)),
            dma((3,)),
        ],
        compiler_params=pltpu.CompilerParams(
            collective_id=0, has_side_effects=True, vmem_limit_bytes=56 * 2**20
        ),
        name="transformer_block",
    )(
        latent,
        ln_gain[0],
        ln_bias[0],
        w_qkv[0].transpose(1, 0, 2).reshape(3 * HD, width),
        w_out[0],
        w_gate[0].T,
        w_value[0].T,
        w_down[0],
    )


def solution(mesh):
    return jax.shard_map(
        per_device,
        mesh=mesh,
        in_specs=(
            P("rows", "cols", None),
            P(),
            P(),
            P(None, "cols", None, None),
            P(None, "cols", None),
            P(None, None, "cols"),
            P(None, None, "cols"),
            P(None, "cols", None),
        ),
        out_specs=P("rows", "cols", None),
        check_vma=False,
    )
```

```python
import math

import jax
import jax.numpy as jnp
from jax import lax
from jax.experimental import pallas as pl
from jax.experimental.pallas import tpu as pltpu
from jax.sharding import PartitionSpec as P

HD = 64
MESH = pl.DeviceIdType.MESH
F32, BF16 = jnp.float32, jnp.bfloat16


def norm_rows(values, gain, bias):
    row_mean = jnp.mean(values, axis=-1, keepdims=True)
    centred = values - row_mean
    row_var = jnp.mean(centred * centred, axis=-1, keepdims=True)
    return (centred * lax.rsqrt(row_var + 1e-05) * gain + bias).astype(BF16)


def dot(left, right, left_dim, right_dim):
    return lax.dot_general(
        left, right, (((left_dim,), (right_dim,)), ((), ())), preferred_element_type=F32
    )


def block_kernel(
    latent, gain_in, bias_in, w_qkv, w_out, w_gate, w_value, w_down, result,
    rows_in, rows_far, gain, bias, tokens, stream, partial, summed, keys, query,
    wkv, wq, wo, wgv, wgv_t, wdown, top, accum, attn_sum, attended, attended_other,
    sem_l, sem_w, sem_wr, sem_or, sem_xr, sem_yr, sem_ar, sem_zr, sem_gr, sem_cr, sem_pr, sem_s,
):
    row, col = lax.axis_index("rows"), lax.axis_index("cols")
    core, me = col % 2, col // 2
    mate = lax.bitwise_xor(core, row % 8 // 4)
    sibling = (row, col + 1 - 2 * core)
    width = gain.shape[1]

    def chip(distance):
        return (row, lax.bitwise_xor(col, 2 * distance))

    def plane(distance):
        return (lax.bitwise_xor(row, distance), col)

    def remote(src, dst, send, recv, device):
        return pltpu.make_async_remote_copy(
            src_ref=src, dst_ref=dst, send_sem=send, recv_sem=recv, device_id=device, device_id_type=MESH
        )

    NEAR, ACROSS, FAR, SHARE, SHARE_FFN, NEAR_KEYS, FAR_KEYS, SIBLING, OUT, FORWARD, RETURN, HEADS, PIECE = range(13)

    def begin(src, dst, kind, recv, device):
        copy = remote(src, dst, sem_s.at[kind], recv, device)
        copy.start()
        return copy

    barrier = pltpu.get_barrier_semaphore()
    pl.semaphore_signal(barrier, inc=1, device_id=plane(4), device_id_type=MESH)
    for distance in range(7, 0, -1):
        pl.semaphore_signal(barrier, inc=1, device_id=chip(distance), device_id_type=MESH)
    for distance in range(1, 4):
        pl.semaphore_signal(barrier, inc=1, device_id=plane(distance), device_id_type=MESH)
    pl.semaphore_signal(barrier, inc=1, device_id=sibling, device_id_type=MESH)

    def begin_local(src, dst, sem):
        copy = pltpu.make_async_copy(src, dst, sem)
        copy.start()
        return copy

    local = [
        begin_local(latent, rows_in.at[me], sem_l.at[0]),
        begin_local(gain_in, gain, sem_l.at[1]),
        begin_local(bias_in, bias, sem_l.at[2]),
    ]
    homes = [
        (w_qkv.at[pl.ds(HD, 2 * HD)], wkv.at[mate], wkv.at[mate]),
        (w_qkv.at[pl.ds(0, HD)], wq.at[mate], wq.at[mate]),
        (w_out, wo.at[0, mate], wo.at[0, mate]),
        (w_gate, wgv.at[0], wgv.at[1]),
        (w_value, wgv.at[2], wgv.at[3]),
        (w_down, wdown.at[0], wdown.at[1]),
    ]
    groups = (0, 0, 1, 2, 2, 3)

    def fetch(first, last):
        for index in range(first, last):
            begin_local(homes[index][0], homes[index][1], sem_w.at[groups[index]])

    def share(first, last, kind):
        for index in range(first, last):
            begin(homes[index][0], homes[index][2], kind, sem_wr.at[groups[index]], sibling)

    def wait_weights(group, whole):
        pltpu.make_async_copy(whole, whole, sem_w.at[group]).wait()
        remote(whole, whole, sem_s.at[SHARE], sem_wr.at[group], sibling).wait_recv()

    fetch(0, 3)
    pl.semaphore_wait(barrier, 12)

    across = [
        begin(latent.at[pl.ds(4 * part, 4)], rows_far.at[me, part], ACROSS, sem_pr.at[part], plane(4))
        for part in range(2)
    ]
    for distance in range(7, 0, -1):
        begin(latent, rows_in.at[me], NEAR, sem_xr.at[distance], chip(distance))
    share(0, 3, SHARE)
    fetch(3, 6)
    share(3, 6, SHARE_FFN)

    def near_copy(distance):
        block = rows_in.at[lax.bitwise_xor(me, distance)]
        return remote(block, block, sem_s.at[NEAR], sem_xr.at[distance], chip(distance))

    def far_copy(part, distance):
        block = rows_far.at[lax.bitwise_xor(me, distance), part]
        return remote(block, block, sem_s.at[FAR], sem_yr.at[part, distance], chip(distance))

    def near_norm(distance):
        slot = lax.bitwise_xor(me, distance)
        for part in range(2):
            rows = rows_in[slot, pl.ds(4 * part, 4)].astype(F32).reshape(16, width)
            stream[part, slot] = rows.astype(BF16)
            tokens[0, part, slot] = norm_rows(rows, gain[0:1, :], bias[0:1, :])

    def near_step(distance, carry):
        near_copy(distance).wait_recv()
        near_norm(distance)
        return carry

    for copy in local:
        copy.wait()
    near_norm(0)
    for part in range(2):
        across[part].wait_recv()
        for distance in range(7, 0, -1):
            mine = rows_far.at[me, part]
            begin(mine, mine, FAR, sem_yr.at[part, distance], chip(distance))
    lax.fori_loop(1, 8, near_step, 0)
    wait_weights(0, w_qkv)

    scale = HD ** (-0.5) * math.log2(math.e)

    def project(which, part):
        piece = tokens[which, part].reshape(128, width)
        place = pl.ds(128 * part, 128)
        keys[4 * which, core, place] = dot(piece, wkv[0], 1, 1).astype(BF16)
        query[0:HD, pl.ds(256 * which + 128 * part, 128)] = (dot(wq[0], piece, 1, 1) * scale).astype(BF16)

    def send_sibling(slot):
        block = keys.at[slot, core]
        begin(block, block, SIBLING, sem_gr.at[slot // 4], sibling)

    def from_sibling(group):
        blocks = keys.at[pl.ds(4 * group, 4), 1 - core]
        remote(blocks, blocks, sem_s.at[SIBLING], sem_gr.at[group], sibling).wait_recv()

    def from_plane(slot):
        block = keys.at[slot, core]
        remote(block, block, sem_s.at[NEAR_KEYS], sem_zr.at[slot], plane(4)).wait_recv()

    for part in range(2):
        project(0, part)
    for distance in range(3, 0, -1):
        begin(keys.at[0, core], keys.at[distance, core], NEAR_KEYS, sem_zr.at[distance], plane(distance))
    send_sibling(0)
    query[HD:, :] = jnp.zeros((HD, 512), BF16)

    def far_step(distance, part):
        @pl.when(distance >= 1)
        def _():
            far_copy(part, distance).wait_recv()

        slot = lax.bitwise_xor(me, distance)
        rows = rows_far[slot, part].astype(F32).reshape(16, width)
        tokens[1, part, slot] = norm_rows(rows, gain[0:1, :], bias[0:1, :])
        return part

    for part in range(2):
        lax.fori_loop(0, 8, far_step, part)
        project(1, part)
        place = pl.ds(128 * part, 128)
        for distance in range(3, 0, -1):
            begin(
                keys.at[4, core, place], keys.at[4 + distance, core, place],
                FAR_KEYS, sem_zr.at[4 + distance], plane(distance),
            )
        if part == 0:
            for distance in range(7, 0, -1):
                begin(w_out, wo.at[distance, mate], OUT, sem_or.at[distance], chip(distance))
    send_sibling(4)

    def scored(block, first, count):
        return dot(block, query[:, first : first + count], 1, 0)

    def summed_values(block, probs):
        lanes = lax.broadcasted_iota(jnp.int32, block.shape, 1)
        return dot(jnp.where(lanes < HD, jnp.ones_like(block), block), probs, 0, 0)

    def fold(block, first, count):
        scores = scored(block, first, count)
        old = top[:, first : first + count]
        new = jnp.maximum(old, jnp.max(scores, axis=0, keepdims=True))
        probs = jnp.exp2(scores - new).astype(BF16)
        accum[:, first : first + count] = accum[:, first : first + count] * jnp.exp2(old - new) + summed_values(block, probs)
        top[:, first : first + count] = new

    def attended_by(first):
        return (accum[HD:, first : first + 256] / accum[0:1, first : first + 256]).astype(BF16)

    for near in range(1, 4):
        from_plane(near)
        send_sibling(near)
    wait_weights(2, wgv.at[pl.ds(0, 2)])
    for index in range(4):
        wgv_t[:, pl.ds(320 * index, 320)] = wgv[index].T
    from_sibling(0)
    block = keys[0:4].reshape(2048, 2 * HD)
    scores = scored(block, 0, 512)
    first_top = jnp.max(scores, axis=0, keepdims=True)
    top[...] = first_top
    accum[...] = summed_values(block, jnp.exp2(scores - first_top).astype(BF16))
    for far in range(5, 8):
        from_plane(far)
        send_sibling(far)
    fold(keys[pl.ds(4, 4), core].reshape(1024, 2 * HD), 256, 256)
    from_sibling(1)
    fold(keys[pl.ds(4, 4), 1 - core].reshape(1024, 2 * HD), 256, 256)
    attended_other[...] = attended_by(256)
    returned = begin(attended_other, attended.at[0, pl.ds(HD, HD)], RETURN, sem_pr.at[2], plane(4))
    fold(keys[4:8].reshape(2048, 2 * HD), 0, 256)

    attended[0, 0:HD] = attended_by(0)
    def spread_heads(part):
        block = pl.ds(HD * part, HD)
        for distance in range(7, 0, -1):
            begin(
                attended.at[0, block], attended.at[distance, block], HEADS, sem_ar.at[part], chip(distance)
            )

    def wait_heads(part):
        blocks = attended.at[pl.ds(1, 7), pl.ds(HD * part, HD)]
        remote(blocks, blocks, sem_s.at[HEADS], sem_ar.at[part], sibling).wait_recv()

    spread_heads(0)
    returned.wait_recv()
    spread_heads(1)
    wait_weights(1, w_out)
    for distance in range(7, 0, -1):
        block = wo.at[distance, mate]
        remote(block, block, sem_s.at[OUT], sem_or.at[distance], chip(distance)).wait_recv()
        begin(block, block, FORWARD, sem_or.at[0], sibling)
    blocks = wo.at[pl.ds(1, 7), 1 - mate]
    remote(blocks, blocks, sem_s.at[FORWARD], sem_or.at[0], sibling).wait_recv()
    wait_heads(0)

    def projected(part):
        heads = attended[:, HD * part : HD * (part + 1)].reshape(8 * HD, 256)
        return dot(heads, wo[:, part].reshape(8 * HD, width), 0, 0)

    attn_sum[...] = projected(0)
    wait_weights(3, w_down)
    wait_heads(1)
    total = stream[...].reshape(256, width).astype(F32) + (attn_sum[...] + projected(1))
    stream[...] = total.astype(BF16).reshape(stream.shape)

    units = wdown.shape[0] * wdown.shape[1]

    def piece(slot):
        return remote(
            partial.at[:, lax.bitwise_xor(me, slot)], summed.at[slot], sem_s.at[PIECE], sem_cr.at[slot], chip(slot)
        )

    def feed(index, carry):
        base = 4 * lax.bitwise_xor(1 - index, me // 4)
        rows = stream[:, pl.ds(base, 4)].reshape(128, width).astype(F32)
        normed = norm_rows(rows, gain[1:2, :], bias[1:2, :])
        sums = dot(normed, wgv_t[...], 1, 0)
        gate, value = sums[:, :units], sums[:, units:]
        hidden = (value * (gate * (lax.erf(gate * (0.5**0.5)) + 1.0) * 0.5)).astype(BF16)
        terms = dot(hidden, wdown[...].reshape(units, width), 1, 0)
        partial[:, pl.ds(base, 4)] = terms.astype(BF16).reshape(2, 4, 16, width)
        for offset in range(3, -1, -1):
            distance = 4 - 4 * index + offset

            @pl.when(distance >= 1)
            def _():
                piece(distance).start()

        return carry

    lax.fori_loop(0, 2, feed, 0)
    total = stream[:, me].astype(F32) + partial[:, me].astype(F32)
    for distance in range(1, 8):
        piece(distance).wait_recv()
        total += summed[distance].astype(F32)
    result[...] = total.reshape(8, 4, width).astype(BF16)

    seven = pl.ds(0, 7)
    three = keys.at[pl.ds(0, 3), 0]
    for kind, sent in (
        (NEAR, rows_in.at[seven]),
        (ACROSS, rows_far.at[0]),
        (FAR, rows_far.at[seven]),
        (SHARE, wkv),
        (SHARE_FFN, wgv.at[pl.ds(0, 3)]),
        (NEAR_KEYS, three),
        (FAR_KEYS, three),
        (SIBLING, keys.at[:, 0]),
        (OUT, wo.at[seven, 0]),
        (FORWARD, wo.at[seven, 0]),
        (RETURN, attended_other),
        (HEADS, attended.at[seven]),
        (PIECE, summed.at[seven]),
    ):
        remote(sent, sent, sem_s.at[kind], sem_pr.at[0], sibling).wait_send()


def per_device(latent, ln_gain, ln_bias, w_qkv, w_out, w_gate, w_value, w_down):
    width = latent.shape[-1]
    own_units = w_gate.shape[2]
    vmem, anywhere = pl.BlockSpec(memory_space=pltpu.VMEM), pl.BlockSpec(memory_space=pl.ANY)
    dma = pltpu.SemaphoreType.DMA
    return pl.pallas_call(
        block_kernel,
        out_shape=pltpu.VMEM(latent.shape, BF16),
        in_specs=[anywhere] * 8,
        out_specs=vmem,
        scratch_shapes=[
            pltpu.VMEM((8, *latent.shape), BF16),
            pltpu.VMEM((8, 2, 4, *latent.shape[1:]), BF16),
            pltpu.VMEM((2, width), F32),
            pltpu.VMEM((2, width), F32),
            pltpu.VMEM((2, 2, 8, 16, width), BF16),
            pltpu.VMEM((2, 8, 16, width), BF16),
            pltpu.VMEM((2, 8, 16, width), BF16),
            pltpu.VMEM((8, 2, 16, width), BF16),
            pltpu.VMEM((8, 2, 256, 2 * HD), BF16),
            pltpu.VMEM((2 * HD, 512), BF16),
            pltpu.VMEM((2, 2 * HD, width), BF16),
            pltpu.VMEM((2, HD, width), BF16),
            pltpu.VMEM((8, 2, HD, width), BF16),
            pltpu.VMEM((4, own_units, width), BF16),
            pltpu.VMEM((width, 4 * own_units), BF16),
            pltpu.VMEM((2, own_units, width), BF16),
            pltpu.VMEM((1, 512), F32),
            pltpu.VMEM((2 * HD, 512), F32),
            pltpu.VMEM((256, width), F32),
            pltpu.VMEM((8, 2 * HD, 256), BF16),
            pltpu.VMEM((HD, 256), BF16),
            dma((3,)),
            dma((4,)),
            dma((4,)),
            dma((8,)),
            dma((8,)),
            dma((2, 8)),
            dma((2,)),
            dma((8,)),
            dma((2,)),
            dma((8,)),
            dma((3,)),
            dma((13,)),
        ],
        compiler_params=pltpu.CompilerParams(
            collective_id=0, has_side_effects=True, vmem_limit_bytes=56 * 2**20
        ),
        name="transformer_block",
    )(
        latent,
        ln_gain[0],
        ln_bias[0],
        w_qkv[0].transpose(1, 0, 2).reshape(3 * HD, width),
        w_out[0],
        w_gate[0].T,
        w_value[0].T,
        w_down[0],
    )


def solution(mesh):
    return jax.shard_map(
        per_device,
        mesh=mesh,
        in_specs=(
            P("rows", "cols", None),
            P(),
            P(),
            P(None, "cols", None, None),
            P(None, "cols", None),
            P(None, None, "cols"),
            P(None, None, "cols"),
            P(None, "cols", None),
        ),
        out_specs=P("rows", "cols", None),
        check_vma=False,
    )
```

```python
import math

import jax
import jax.numpy as jnp
from jax import lax
from jax.experimental import pallas as pl
from jax.experimental.pallas import tpu as pltpu
from jax.sharding import PartitionSpec as P

HD = 64
MESH = pl.DeviceIdType.MESH
F32, BF16 = jnp.float32, jnp.bfloat16


def norm_rows(values, gain, bias):
    row_mean = jnp.mean(values, axis=-1, keepdims=True)
    centred = values - row_mean
    row_var = jnp.mean(centred * centred, axis=-1, keepdims=True)
    return (centred * lax.rsqrt(row_var + 1e-05) * gain + bias).astype(BF16)


def dot(left, right, left_dim, right_dim):
    return lax.dot_general(
        left, right, (((left_dim,), (right_dim,)), ((), ())), preferred_element_type=F32
    )


def block_kernel(
    latent, gain_in, bias_in, w_qkv, w_out, w_gate, w_value, w_down, result,
    rows_in, rows_far, gain, bias, tokens, stream, partial, summed, keys, query,
    wkv, wq, wo, wgv, wgv_t, wdown, top, accum, attn_sum, attended, attended_other,
    sem_l, sem_w, sem_wr, sem_or, sem_xr, sem_yr, sem_ar, sem_zr, sem_gr, sem_cr, sem_pr, sem_s,
):
    row, col = lax.axis_index("rows"), lax.axis_index("cols")
    core, me = col % 2, col // 2
    mate = lax.bitwise_xor(core, row % 8 // 4)
    sibling = (row, col + 1 - 2 * core)
    width = gain.shape[1]

    def chip(distance):
        return (row, lax.bitwise_xor(col, 2 * distance))

    def plane(distance):
        return (lax.bitwise_xor(row, distance), col)

    def remote(src, dst, send, recv, device):
        return pltpu.make_async_remote_copy(
            src_ref=src, dst_ref=dst, send_sem=send, recv_sem=recv, device_id=device, device_id_type=MESH
        )

    NEAR, ACROSS, FAR, SHARE, SHARE_FFN, NEAR_KEYS, FAR_KEYS, SIBLING, OUT, FORWARD, RETURN, HEADS, PIECE = range(13)

    def begin(src, dst, kind, recv, device):
        copy = remote(src, dst, sem_s.at[kind], recv, device)
        copy.start()
        return copy

    barrier = pltpu.get_barrier_semaphore()
    pl.semaphore_signal(barrier, inc=1, device_id=plane(4), device_id_type=MESH)
    for distance in range(7, 0, -1):
        pl.semaphore_signal(barrier, inc=1, device_id=chip(distance), device_id_type=MESH)
    for distance in range(1, 4):
        pl.semaphore_signal(barrier, inc=1, device_id=plane(distance), device_id_type=MESH)
    pl.semaphore_signal(barrier, inc=1, device_id=sibling, device_id_type=MESH)

    def begin_local(src, dst, sem):
        copy = pltpu.make_async_copy(src, dst, sem)
        copy.start()
        return copy

    local = [
        begin_local(latent, rows_in.at[me], sem_l.at[0]),
        begin_local(gain_in, gain, sem_l.at[1]),
        begin_local(bias_in, bias, sem_l.at[2]),
    ]
    homes = [
        (w_qkv.at[pl.ds(HD, 2 * HD)], wkv.at[mate], wkv.at[mate]),
        (w_qkv.at[pl.ds(0, HD)], wq.at[mate], wq.at[mate]),
        (w_out, wo.at[0, mate], wo.at[0, mate]),
        (w_gate, wgv.at[0], wgv.at[1]),
        (w_value, wgv.at[2], wgv.at[3]),
        (w_down, wdown.at[0], wdown.at[1]),
    ]
    groups = (0, 0, 1, 2, 2, 3)

    def fetch(first, last):
        for index in range(first, last):
            begin_local(homes[index][0], homes[index][1], sem_w.at[groups[index]])

    def share(first, last, kind):
        for index in range(first, last):
            begin(homes[index][0], homes[index][2], kind, sem_wr.at[groups[index]], sibling)

    def wait_weights(group, whole):
        pltpu.make_async_copy(whole, whole, sem_w.at[group]).wait()
        remote(whole, whole, sem_s.at[SHARE], sem_wr.at[group], sibling).wait_recv()

    fetch(0, 3)
    pl.semaphore_wait(barrier, 12)

    across = [
        begin(latent.at[pl.ds(4 * part, 4)], rows_far.at[me, part], ACROSS, sem_pr.at[part], plane(4))
        for part in range(2)
    ]
    for distance in range(7, 0, -1):
        begin(latent, rows_in.at[me], NEAR, sem_xr.at[distance], chip(distance))
    share(0, 3, SHARE)
    fetch(3, 6)
    share(3, 6, SHARE_FFN)

    def spread_out(rows):
        for distance in range(7, 0, -1):
            begin(w_out.at[rows], wo.at[distance, mate, rows], OUT, sem_or.at[distance], chip(distance))

    spread_out(pl.ds(0, 16))

    def near_copy(distance):
        block = rows_in.at[lax.bitwise_xor(me, distance)]
        return remote(block, block, sem_s.at[NEAR], sem_xr.at[distance], chip(distance))

    def far_copy(part, distance):
        block = rows_far.at[lax.bitwise_xor(me, distance), part]
        return remote(block, block, sem_s.at[FAR], sem_yr.at[part, distance], chip(distance))

    def near_norm(distance):
        slot = lax.bitwise_xor(me, distance)
        for part in range(2):
            rows = rows_in[slot, pl.ds(4 * part, 4)].astype(F32).reshape(16, width)
            stream[part, slot] = rows.astype(BF16)
            tokens[0, part, slot] = norm_rows(rows, gain[0:1, :], bias[0:1, :])

    def near_step(distance, carry):
        near_copy(distance).wait_recv()
        near_norm(distance)
        return carry

    for copy in local:
        copy.wait()
    near_norm(0)
    for part in range(2):
        across[part].wait_recv()
        for distance in range(7, 0, -1):
            mine = rows_far.at[me, part]
            begin(mine, mine, FAR, sem_yr.at[part, distance], chip(distance))
    lax.fori_loop(1, 8, near_step, 0)
    wait_weights(0, w_qkv)

    scale = HD ** (-0.5) * math.log2(math.e)

    def project(which, part):
        piece = tokens[which, part].reshape(128, width)
        place = pl.ds(128 * part, 128)
        keys[4 * which, core, place] = dot(piece, wkv[0], 1, 1).astype(BF16)
        query[0:HD, pl.ds(256 * which + 128 * part, 128)] = (dot(wq[0], piece, 1, 1) * scale).astype(BF16)

    def send_sibling(slot):
        block = keys.at[slot, core]
        begin(block, block, SIBLING, sem_gr.at[slot // 4], sibling)

    def from_sibling(group):
        blocks = keys.at[pl.ds(4 * group, 4), 1 - core]
        remote(blocks, blocks, sem_s.at[SIBLING], sem_gr.at[group], sibling).wait_recv()

    def from_plane(slot):
        block = keys.at[slot, core]
        remote(block, block, sem_s.at[NEAR_KEYS], sem_zr.at[slot], plane(4)).wait_recv()

    for part in range(2):
        project(0, part)
    for distance in range(3, 0, -1):
        begin(keys.at[0, core], keys.at[distance, core], NEAR_KEYS, sem_zr.at[distance], plane(distance))
    send_sibling(0)
    query[HD:, :] = jnp.zeros((HD, 512), BF16)

    def far_step(distance, part):
        @pl.when(distance >= 1)
        def _():
            far_copy(part, distance).wait_recv()

        slot = lax.bitwise_xor(me, distance)
        rows = rows_far[slot, part].astype(F32).reshape(16, width)
        tokens[1, part, slot] = norm_rows(rows, gain[0:1, :], bias[0:1, :])
        return part

    for part in range(2):
        lax.fori_loop(0, 8, far_step, part)
        project(1, part)
        place = pl.ds(128 * part, 128)
        for distance in range(3, 0, -1):
            begin(
                keys.at[4, core, place], keys.at[4 + distance, core, place],
                FAR_KEYS, sem_zr.at[4 + distance], plane(distance),
            )
    send_sibling(4)
    spread_out(pl.ds(16, 48))

    def scored(block, first, count):
        return dot(block, query[:, first : first + count], 1, 0)

    def summed_values(block, probs):
        lanes = lax.broadcasted_iota(jnp.int32, block.shape, 1)
        return dot(jnp.where(lanes < HD, jnp.ones_like(block), block), probs, 0, 0)

    def fold(block, first, count):
        scores = scored(block, first, count)
        old = top[:, first : first + count]
        new = jnp.maximum(old, jnp.max(scores, axis=0, keepdims=True))
        probs = jnp.exp2(scores - new).astype(BF16)
        accum[:, first : first + count] = accum[:, first : first + count] * jnp.exp2(old - new) + summed_values(block, probs)
        top[:, first : first + count] = new

    def attended_by(first):
        return (accum[HD:, first : first + 256] / accum[0:1, first : first + 256]).astype(BF16)

    for near in range(1, 4):
        from_plane(near)
        send_sibling(near)
    wait_weights(2, wgv.at[pl.ds(0, 2)])
    for index in range(4):
        wgv_t[:, pl.ds(320 * index, 320)] = wgv[index].T
    from_sibling(0)
    block = keys[0:4].reshape(2048, 2 * HD)
    scores = scored(block, 0, 512)
    first_top = jnp.max(scores, axis=0, keepdims=True)
    top[...] = first_top
    accum[...] = summed_values(block, jnp.exp2(scores - first_top).astype(BF16))
    for far in range(5, 8):
        from_plane(far)
        send_sibling(far)
    fold(keys[pl.ds(4, 4), core].reshape(1024, 2 * HD), 256, 256)
    from_sibling(1)
    fold(keys[pl.ds(4, 4), 1 - core].reshape(1024, 2 * HD), 256, 256)
    attended_other[...] = attended_by(256)
    returned = begin(attended_other, attended.at[0, pl.ds(HD, HD)], RETURN, sem_pr.at[2], plane(4))
    fold(keys[4:8].reshape(2048, 2 * HD), 0, 256)

    attended[0, 0:HD] = attended_by(0)
    def spread_heads(part):
        block = pl.ds(HD * part, HD)
        for distance in range(7, 0, -1):
            begin(
                attended.at[0, block], attended.at[distance, block], HEADS, sem_ar.at[part], chip(distance)
            )

    def wait_heads(part):
        blocks = attended.at[pl.ds(1, 7), pl.ds(HD * part, HD)]
        remote(blocks, blocks, sem_s.at[HEADS], sem_ar.at[part], sibling).wait_recv()

    spread_heads(0)
    returned.wait_recv()
    spread_heads(1)
    wait_weights(1, w_out)
    for distance in range(7, 0, -1):
        block = wo.at[distance, mate]
        remote(block, block, sem_s.at[OUT], sem_or.at[distance], chip(distance)).wait_recv()
        begin(block, block, FORWARD, sem_or.at[0], sibling)
    blocks = wo.at[pl.ds(1, 7), 1 - mate]
    remote(blocks, blocks, sem_s.at[FORWARD], sem_or.at[0], sibling).wait_recv()
    wait_heads(0)

    def projected(part):
        heads = attended[:, HD * part : HD * (part + 1)].reshape(8 * HD, 256)
        return dot(heads, wo[:, part].reshape(8 * HD, width), 0, 0)

    attn_sum[...] = projected(0)
    wait_weights(3, w_down)
    wait_heads(1)
    total = stream[...].reshape(256, width).astype(F32) + (attn_sum[...] + projected(1))
    stream[...] = total.astype(BF16).reshape(stream.shape)

    units = wdown.shape[0] * wdown.shape[1]

    def piece(slot):
        return remote(
            partial.at[:, lax.bitwise_xor(me, slot)], summed.at[slot], sem_s.at[PIECE], sem_cr.at[slot], chip(slot)
        )

    def feed(index, carry):
        base = 4 * lax.bitwise_xor(1 - index, me // 4)
        rows = stream[:, pl.ds(base, 4)].reshape(128, width).astype(F32)
        normed = norm_rows(rows, gain[1:2, :], bias[1:2, :])
        sums = dot(normed, wgv_t[...], 1, 0)
        gate, value = sums[:, :units], sums[:, units:]
        hidden = (value * (gate * (lax.erf(gate * (0.5**0.5)) + 1.0) * 0.5)).astype(BF16)
        terms = dot(hidden, wdown[...].reshape(units, width), 1, 0)
        partial[:, pl.ds(base, 4)] = terms.astype(BF16).reshape(2, 4, 16, width)
        for offset in range(3, -1, -1):
            distance = 4 - 4 * index + offset

            @pl.when(distance >= 1)
            def _():
                piece(distance).start()

        return carry

    lax.fori_loop(0, 2, feed, 0)
    total = stream[:, me].astype(F32) + partial[:, me].astype(F32)
    for distance in range(1, 8):
        piece(distance).wait_recv()
        total += summed[distance].astype(F32)
    result[...] = total.reshape(8, 4, width).astype(BF16)

    seven = pl.ds(0, 7)
    three = keys.at[pl.ds(0, 3), 0]
    for kind, sent in (
        (NEAR, rows_in.at[seven]),
        (ACROSS, rows_far.at[0]),
        (FAR, rows_far.at[seven]),
        (SHARE, wkv),
        (SHARE_FFN, wgv.at[pl.ds(0, 3)]),
        (NEAR_KEYS, three),
        (FAR_KEYS, three),
        (SIBLING, keys.at[:, 0]),
        (OUT, wo.at[seven, 0]),
        (FORWARD, wo.at[seven, 0]),
        (RETURN, attended_other),
        (HEADS, attended.at[seven]),
        (PIECE, summed.at[seven]),
    ):
        remote(sent, sent, sem_s.at[kind], sem_pr.at[0], sibling).wait_send()


def per_device(latent, ln_gain, ln_bias, w_qkv, w_out, w_gate, w_value, w_down):
    width = latent.shape[-1]
    own_units = w_gate.shape[2]
    vmem, anywhere = pl.BlockSpec(memory_space=pltpu.VMEM), pl.BlockSpec(memory_space=pl.ANY)
    dma = pltpu.SemaphoreType.DMA
    return pl.pallas_call(
        block_kernel,
        out_shape=pltpu.VMEM(latent.shape, BF16),
        in_specs=[anywhere] * 8,
        out_specs=vmem,
        scratch_shapes=[
            pltpu.VMEM((8, *latent.shape), BF16),
            pltpu.VMEM((8, 2, 4, *latent.shape[1:]), BF16),
            pltpu.VMEM((2, width), F32),
            pltpu.VMEM((2, width), F32),
            pltpu.VMEM((2, 2, 8, 16, width), BF16),
            pltpu.VMEM((2, 8, 16, width), BF16),
            pltpu.VMEM((2, 8, 16, width), BF16),
            pltpu.VMEM((8, 2, 16, width), BF16),
            pltpu.VMEM((8, 2, 256, 2 * HD), BF16),
            pltpu.VMEM((2 * HD, 512), BF16),
            pltpu.VMEM((2, 2 * HD, width), BF16),
            pltpu.VMEM((2, HD, width), BF16),
            pltpu.VMEM((8, 2, HD, width), BF16),
            pltpu.VMEM((4, own_units, width), BF16),
            pltpu.VMEM((width, 4 * own_units), BF16),
            pltpu.VMEM((2, own_units, width), BF16),
            pltpu.VMEM((1, 512), F32),
            pltpu.VMEM((2 * HD, 512), F32),
            pltpu.VMEM((256, width), F32),
            pltpu.VMEM((8, 2 * HD, 256), BF16),
            pltpu.VMEM((HD, 256), BF16),
            dma((3,)),
            dma((4,)),
            dma((4,)),
            dma((8,)),
            dma((8,)),
            dma((2, 8)),
            dma((2,)),
            dma((8,)),
            dma((2,)),
            dma((8,)),
            dma((3,)),
            dma((13,)),
        ],
        compiler_params=pltpu.CompilerParams(
            collective_id=0, has_side_effects=True, vmem_limit_bytes=56 * 2**20
        ),
        name="transformer_block",
    )(
        latent,
        ln_gain[0],
        ln_bias[0],
        w_qkv[0].transpose(1, 0, 2).reshape(3 * HD, width),
        w_out[0],
        w_gate[0].T,
        w_value[0].T,
        w_down[0],
    )


def solution(mesh):
    return jax.shard_map(
        per_device,
        mesh=mesh,
        in_specs=(
            P("rows", "cols", None),
            P(),
            P(),
            P(None, "cols", None, None),
            P(None, "cols", None),
            P(None, None, "cols"),
            P(None, None, "cols"),
            P(None, "cols", None),
        ),
        out_specs=P("rows", "cols", None),
        check_vma=False,
    )
```

```python
import math

import jax
import jax.numpy as jnp
from jax import lax
from jax.experimental import pallas as pl
from jax.experimental.pallas import tpu as pltpu
from jax.sharding import PartitionSpec as P

HD = 64
MESH = pl.DeviceIdType.MESH
F32, BF16 = jnp.float32, jnp.bfloat16


def norm_rows(values, gain, bias):
    row_mean = jnp.mean(values, axis=-1, keepdims=True)
    centred = values - row_mean
    row_var = jnp.mean(centred * centred, axis=-1, keepdims=True)
    return (centred * lax.rsqrt(row_var + 1e-05) * gain + bias).astype(BF16)


def dot(left, right, left_dim, right_dim):
    return lax.dot_general(
        left, right, (((left_dim,), (right_dim,)), ((), ())), preferred_element_type=F32
    )


def block_kernel(
    latent, gain_in, bias_in, w_qkv, w_out, w_gate, w_value, w_down, result,
    rows_in, rows_far, gain, bias, tokens, stream, partial, summed, keys, query,
    wkv, wq, wo, wgv, wgv_t, wdown, top, accum, attn_sum, attended, attended_other,
    sem_l, sem_w, sem_wr, sem_or, sem_xr, sem_yr, sem_ar, sem_zr, sem_gr, sem_cr, sem_pr, sem_s,
):
    row, col = lax.axis_index("rows"), lax.axis_index("cols")
    core, me = col % 2, col // 2
    mate = lax.bitwise_xor(core, row % 8 // 4)
    sibling = (row, col + 1 - 2 * core)
    width = gain.shape[1]

    def chip(distance):
        return (row, lax.bitwise_xor(col, 2 * distance))

    def plane(distance):
        return (lax.bitwise_xor(row, distance), col)

    def remote(src, dst, send, recv, device):
        return pltpu.make_async_remote_copy(
            src_ref=src, dst_ref=dst, send_sem=send, recv_sem=recv, device_id=device, device_id_type=MESH
        )

    NEAR, ACROSS, FAR, SHARE, SHARE_FFN, NEAR_KEYS, FAR_KEYS, SIBLING, OUT, FORWARD, RETURN, HEADS, PIECE, EXCHANGE = range(14)

    def begin(src, dst, kind, recv, device):
        copy = remote(src, dst, sem_s.at[kind], recv, device)
        copy.start()
        return copy

    barrier = pltpu.get_barrier_semaphore()
    pl.semaphore_signal(barrier, inc=1, device_id=plane(4), device_id_type=MESH)
    for distance in range(7, 0, -1):
        pl.semaphore_signal(barrier, inc=1, device_id=chip(distance), device_id_type=MESH)
    for distance in range(1, 4):
        pl.semaphore_signal(barrier, inc=1, device_id=plane(distance), device_id_type=MESH)
    pl.semaphore_signal(barrier, inc=1, device_id=sibling, device_id_type=MESH)

    def begin_local(src, dst, sem):
        copy = pltpu.make_async_copy(src, dst, sem)
        copy.start()
        return copy

    local = [
        begin_local(latent, rows_in.at[me], sem_l.at[0]),
        begin_local(gain_in, gain, sem_l.at[1]),
        begin_local(bias_in, bias, sem_l.at[2]),
    ]
    homes = [
        (w_qkv.at[pl.ds(HD, 2 * HD)], wkv.at[mate], wkv.at[mate]),
        (w_qkv.at[pl.ds(0, HD)], wq.at[mate], wq.at[mate]),
        (w_out, wo.at[0, mate], wo.at[0, mate]),
        (w_gate, wgv.at[0], wgv.at[1]),
        (w_value, wgv.at[2], wgv.at[3]),
        (w_down, wdown.at[0], wdown.at[1]),
    ]
    groups = (0, 0, 1, 2, 2, 3)

    def fetch(first, last):
        for index in range(first, last):
            begin_local(homes[index][0], homes[index][1], sem_w.at[groups[index]])

    def share(first, last, kind):
        for index in range(first, last):
            begin(homes[index][0], homes[index][2], kind, sem_wr.at[groups[index]], sibling)

    def wait_weights(group, whole):
        pltpu.make_async_copy(whole, whole, sem_w.at[group]).wait()
        remote(whole, whole, sem_s.at[SHARE], sem_wr.at[group], sibling).wait_recv()

    fetch(0, 3)
    pl.semaphore_wait(barrier, 12)

    def quarter(slot, index):
        return rows_far.at[slot, index // 2, pl.ds(2 * (index % 2), 2)]

    across = [
        begin(latent.at[pl.ds(2 * index, 2)], quarter(me, index), ACROSS, sem_pr.at[index], plane(4))
        for index in range(4)
    ]
    for distance in range(7, 0, -1):
        begin(latent, rows_in.at[me], NEAR, sem_xr.at[distance], chip(distance))
    share(0, 3, SHARE)
    fetch(3, 6)
    share(3, 6, SHARE_FFN)

    def spread_out(rows):
        for distance in range(7, 0, -1):
            begin(w_out.at[rows], wo.at[distance, mate, rows], OUT, sem_or.at[distance], chip(distance))

    def near_copy(distance):
        block = rows_in.at[lax.bitwise_xor(me, distance)]
        return remote(block, block, sem_s.at[NEAR], sem_xr.at[distance], chip(distance))

    def far_copy(part, distance):
        block = rows_far.at[lax.bitwise_xor(me, distance), part]
        return remote(block, block, sem_s.at[FAR], sem_yr.at[part, distance], chip(distance))

    def near_norm(distance):
        slot = lax.bitwise_xor(me, distance)
        for part in range(2):
            rows = rows_in[slot, pl.ds(4 * part, 4)].astype(F32).reshape(16, width)
            stream[part, slot] = rows.astype(BF16)
            tokens[0, part, slot] = norm_rows(rows, gain[0:1, :], bias[0:1, :])

    def near_step(distance, carry):
        near_copy(distance).wait_recv()
        near_norm(distance)
        return carry

    for copy in local:
        copy.wait()
    near_norm(0)
    for index in range(4):
        across[index].wait_recv()
        for distance in range(7, 0, -1):
            mine = quarter(me, index)
            begin(mine, mine, FAR, sem_yr.at[index // 2, distance], chip(distance))
    spread_out(pl.ds(0, 16))
    lax.fori_loop(1, 8, near_step, 0)
    wait_weights(0, w_qkv)

    scale = HD ** (-0.5) * math.log2(math.e)

    def project(which, part):
        piece = tokens[which, part].reshape(128, width)
        place = pl.ds(128 * part, 128)
        keys[4 * which, core, place] = dot(piece, wkv[0], 1, 1).astype(BF16)
        query[0:HD, pl.ds(256 * which + 128 * part, 128)] = (dot(wq[0], piece, 1, 1) * scale).astype(BF16)

    def send_sibling(slot):
        block = keys.at[slot, core]
        begin(block, block, SIBLING, sem_gr.at[slot // 4], sibling)

    def from_sibling(group):
        blocks = keys.at[pl.ds(4 * group, 4), 1 - core]
        remote(blocks, blocks, sem_s.at[SIBLING], sem_gr.at[group], sibling).wait_recv()

    def from_plane(slot):
        block = keys.at[slot, core]
        remote(block, block, sem_s.at[NEAR_KEYS], sem_zr.at[slot], plane(4)).wait_recv()

    for part in range(2):
        project(0, part)
    for distance in range(3, 0, -1):
        begin(keys.at[0, core], keys.at[distance, core], NEAR_KEYS, sem_zr.at[distance], plane(distance))
    send_sibling(0)
    query[HD:, :] = jnp.zeros((HD, 512), BF16)

    def far_step(distance, part):
        @pl.when(distance >= 1)
        def _():
            far_copy(part, distance).wait_recv()

        slot = lax.bitwise_xor(me, distance)
        rows = rows_far[slot, part].astype(F32).reshape(16, width)
        tokens[1, part, slot] = norm_rows(rows, gain[0:1, :], bias[0:1, :])
        return part

    for part in range(2):
        lax.fori_loop(0, 8, far_step, part)
        project(1, part)
        place = pl.ds(128 * part, 128)
        for distance in range(3, 0, -1):
            begin(
                keys.at[4, core, place], keys.at[4 + distance, core, place],
                FAR_KEYS, sem_zr.at[4 + distance], plane(distance),
            )
    send_sibling(4)
    spread_out(pl.ds(16, 48))

    def scored(block, first, count):
        return dot(block, query[:, first : first + count], 1, 0)

    def summed_values(block, probs):
        lanes = lax.broadcasted_iota(jnp.int32, block.shape, 1)
        return dot(jnp.where(lanes < HD, jnp.ones_like(block), block), probs, 0, 0)

    def fold(block, first, count):
        scores = scored(block, first, count)
        old = top[:, first : first + count]
        new = jnp.maximum(old, jnp.max(scores, axis=0, keepdims=True))
        probs = jnp.exp2(scores - new).astype(BF16)
        accum[:, first : first + count] = accum[:, first : first + count] * jnp.exp2(old - new) + summed_values(block, probs)
        top[:, first : first + count] = new

    def attended_by(first):
        return (accum[HD:, first : first + 256] / accum[0:1, first : first + 256]).astype(BF16)

    for near in range(1, 4):
        from_plane(near)
        send_sibling(near)
    wait_weights(2, wgv.at[pl.ds(0, 2)])
    for index in range(4):
        wgv_t[:, pl.ds(320 * index, 320)] = wgv[index].T
    from_sibling(0)
    block = keys[0:4].reshape(2048, 2 * HD)
    scores = scored(block, 0, 512)
    first_top = jnp.max(scores, axis=0, keepdims=True)
    top[...] = first_top
    accum[...] = summed_values(block, jnp.exp2(scores - first_top).astype(BF16))
    for far in range(5, 8):
        from_plane(far)
        send_sibling(far)
    fold(keys[pl.ds(4, 4), core].reshape(1024, 2 * HD), 256, 256)
    from_sibling(1)
    fold(keys[pl.ds(4, 4), 1 - core].reshape(1024, 2 * HD), 256, 256)
    attended_other[...] = attended_by(256)
    returned = begin(attended_other, attended.at[0, pl.ds(HD, HD)], RETURN, sem_pr.at[4], plane(4))
    fold(keys[4:8].reshape(2048, 2 * HD), 0, 256)

    attended[0, 0:HD] = attended_by(0)
    def spread_heads(group, block):
        for distance in range(7, 0, -1):
            begin(attended.at[0, *block], attended.at[distance, *block], HEADS, sem_ar.at[group], chip(distance))

    def wait_heads(group, block):
        blocks = attended.at[pl.ds(1, 7), *block]
        remote(blocks, blocks, sem_s.at[HEADS], sem_ar.at[group], sibling).wait_recv()

    first_heads = (pl.ds(0, HD), pl.ds(0, 256))

    def later_heads(part):
        return pl.ds(HD, HD), pl.ds(pl.multiple_of(128 * part, 128), 128)

    spread_heads(0, first_heads)
    returned.wait_recv()
    for part in range(2):
        spread_heads(1 + part, later_heads(part))
    wait_weights(1, w_out)
    for distance in range(7, 0, -1):
        block = wo.at[distance, mate]
        remote(block, block, sem_s.at[OUT], sem_or.at[distance], chip(distance)).wait_recv()
        begin(block, block, FORWARD, sem_or.at[0], sibling)
    blocks = wo.at[pl.ds(1, 7), 1 - mate]
    remote(blocks, blocks, sem_s.at[FORWARD], sem_or.at[0], sibling).wait_recv()
    wait_heads(0, first_heads)

    heads = attended[:, :HD].reshape(8 * HD, 256)
    attn_sum[...] = dot(heads, wo[:, 0].reshape(8 * HD, width), 0, 0).reshape(attn_sum.shape)
    wait_weights(3, w_down)

    units = wdown.shape[0] * wdown.shape[1]

    def piece(slot, part):
        return remote(
            partial.at[part, lax.bitwise_xor(me, slot)], summed.at[slot, part],
            sem_s.at[PIECE], sem_cr.at[slot], chip(slot),
        )

    def feed(part, carry):
        wait_heads(1 + part, later_heads(part))
        heads = attended[:, HD:, pl.ds(pl.multiple_of(128 * part, 128), 128)].reshape(8 * HD, 128)
        added = attn_sum[part] + dot(heads, wo[:, 1].reshape(8 * HD, width), 0, 0)
        rounded = (stream[part].reshape(128, width).astype(F32) + added).astype(BF16)
        stream[part] = rounded.reshape(8, 16, width)
        rows = rounded.astype(F32)
        normed = norm_rows(rows, gain[1:2, :], bias[1:2, :])
        sums = dot(normed, wgv_t[...], 1, 0)
        gate, value = sums[:, :units], sums[:, units:]
        hidden = (value * (gate * (lax.erf(gate * (0.5**0.5)) + 1.0) * 0.5)).astype(BF16)
        terms = dot(hidden, wdown[...].reshape(units, width), 1, 0)
        partial[part] = terms.astype(BF16).reshape(8, 16, width)
        for distance in range(7, 0, -1):
            piece(distance, part).start()
        return carry

    lax.fori_loop(0, 2, feed, 0)
    total = stream[:, me].astype(F32) + partial[:, me].astype(F32)
    for distance in range(1, 8):
        block = summed.at[distance]
        remote(block, block, sem_s.at[PIECE], sem_cr.at[distance], sibling).wait_recv()
        total += summed[distance].astype(F32)
    result[...] = total.reshape(8, 4, width).astype(BF16)

    seven = pl.ds(0, 7)
    three = keys.at[pl.ds(0, 3), 0]
    for kind, sent in (
        (NEAR, rows_in.at[seven]),
        (ACROSS, rows_far.at[0]),
        (FAR, rows_far.at[seven]),
        (SHARE, wkv),
        (SHARE_FFN, wgv.at[pl.ds(0, 3)]),
        (NEAR_KEYS, three),
        (FAR_KEYS, three),
        (SIBLING, keys.at[:, 0]),
        (OUT, wo.at[seven, 0]),
        (FORWARD, wo.at[seven, 0]),
        (RETURN, attended_other),
        (HEADS, attended.at[seven]),
        (PIECE, summed.at[seven]),
    ):
        remote(sent, sent, sem_s.at[kind], sem_pr.at[0], sibling).wait_send()


def per_device(latent, ln_gain, ln_bias, w_qkv, w_out, w_gate, w_value, w_down):
    width = latent.shape[-1]
    own_units = w_gate.shape[2]
    vmem, anywhere = pl.BlockSpec(memory_space=pltpu.VMEM), pl.BlockSpec(memory_space=pl.ANY)
    dma = pltpu.SemaphoreType.DMA
    return pl.pallas_call(
        block_kernel,
        out_shape=pltpu.VMEM(latent.shape, BF16),
        in_specs=[anywhere] * 8,
        out_specs=vmem,
        scratch_shapes=[
            pltpu.VMEM((8, *latent.shape), BF16),
            pltpu.VMEM((8, 2, 4, *latent.shape[1:]), BF16),
            pltpu.VMEM((2, width), F32),
            pltpu.VMEM((2, width), F32),
            pltpu.VMEM((2, 2, 8, 16, width), BF16),
            pltpu.VMEM((2, 8, 16, width), BF16),
            pltpu.VMEM((2, 8, 16, width), BF16),
            pltpu.VMEM((8, 2, 16, width), BF16),
            pltpu.VMEM((8, 2, 256, 2 * HD), BF16),
            pltpu.VMEM((2 * HD, 512), BF16),
            pltpu.VMEM((2, 2 * HD, width), BF16),
            pltpu.VMEM((2, HD, width), BF16),
            pltpu.VMEM((8, 2, HD, width), BF16),
            pltpu.VMEM((4, own_units, width), BF16),
            pltpu.VMEM((width, 4 * own_units), BF16),
            pltpu.VMEM((2, own_units, width), BF16),
            pltpu.VMEM((1, 512), F32),
            pltpu.VMEM((2 * HD, 512), F32),
            pltpu.VMEM((2, 128, width), F32),
            pltpu.VMEM((8, 2 * HD, 256), BF16),
            pltpu.VMEM((HD, 256), BF16),
            dma((3,)),
            dma((4,)),
            dma((4,)),
            dma((8,)),
            dma((8,)),
            dma((2, 8)),
            dma((3,)),
            dma((8,)),
            dma((2,)),
            dma((8,)),
            dma((5,)),
            dma((14,)),
        ],
        compiler_params=pltpu.CompilerParams(
            collective_id=0, has_side_effects=True, vmem_limit_bytes=56 * 2**20
        ),
        name="transformer_block",
    )(
        latent,
        ln_gain[0],
        ln_bias[0],
        w_qkv[0].transpose(1, 0, 2).reshape(3 * HD, width),
        w_out[0],
        w_gate[0].T,
        w_value[0].T,
        w_down[0],
    )


def solution(mesh):
    return jax.shard_map(
        per_device,
        mesh=mesh,
        in_specs=(
            P("rows", "cols", None),
            P(),
            P(),
            P(None, "cols", None, None),
            P(None, "cols", None),
            P(None, None, "cols"),
            P(None, None, "cols"),
            P(None, "cols", None),
        ),
        out_specs=P("rows", "cols", None),
        check_vma=False,
    )
```

```python
import math

import jax
import jax.numpy as jnp
from jax import lax
from jax.experimental import pallas as pl
from jax.experimental.pallas import tpu as pltpu
from jax.sharding import PartitionSpec as P

HD = 64
MESH = pl.DeviceIdType.MESH
F32, BF16 = jnp.float32, jnp.bfloat16


def norm_rows(values, gain, bias):
    row_mean = jnp.mean(values, axis=-1, keepdims=True)
    centred = values - row_mean
    row_var = jnp.mean(centred * centred, axis=-1, keepdims=True)
    return (centred * lax.rsqrt(row_var + 1e-05) * gain + bias).astype(BF16)


def dot(left, right, left_dim, right_dim):
    return lax.dot_general(
        left, right, (((left_dim,), (right_dim,)), ((), ())), preferred_element_type=F32
    )


def block_kernel(
    latent, gain_in, bias_in, w_qkv, w_out, w_gate, w_value, w_down, result,
    rows_in, rows_far, gain, bias, tokens, stream, partial, summed, keys, query,
    wkv, wq, wo, wgv, wgv_t, wdown, top, accum, attn_sum, attended, attended_other,
    sem_l, sem_w, sem_wr, sem_or, sem_xr, sem_yr, sem_ar, sem_zr, sem_gr, sem_cr, sem_pr, sem_s,
):
    row, col = lax.axis_index("rows"), lax.axis_index("cols")
    core, me = col % 2, col // 2
    mate = lax.bitwise_xor(core, row % 8 // 4)
    sibling = (row, col + 1 - 2 * core)
    width = gain.shape[1]

    def chip(distance):
        return (row, lax.bitwise_xor(col, 2 * distance))

    def plane(distance):
        return (lax.bitwise_xor(row, distance), col)

    def remote(src, dst, send, recv, device):
        return pltpu.make_async_remote_copy(
            src_ref=src, dst_ref=dst, send_sem=send, recv_sem=recv, device_id=device, device_id_type=MESH
        )

    NEAR, ACROSS, FAR, SHARE, SHARE_FFN, NEAR_KEYS, FAR_KEYS, SIBLING, OUT, FORWARD, RETURN, HEADS, PIECE, EXCHANGE = range(14)

    def begin(src, dst, kind, recv, device):
        copy = remote(src, dst, sem_s.at[kind], recv, device)
        copy.start()
        return copy

    barrier = pltpu.get_barrier_semaphore()
    pl.semaphore_signal(barrier, inc=1, device_id=plane(4), device_id_type=MESH)
    for distance in range(7, 0, -1):
        pl.semaphore_signal(barrier, inc=1, device_id=chip(distance), device_id_type=MESH)
    for distance in range(1, 4):
        pl.semaphore_signal(barrier, inc=1, device_id=plane(distance), device_id_type=MESH)
    pl.semaphore_signal(barrier, inc=1, device_id=sibling, device_id_type=MESH)

    def begin_local(src, dst, sem):
        copy = pltpu.make_async_copy(src, dst, sem)
        copy.start()
        return copy

    local = [
        begin_local(latent, rows_in.at[me], sem_l.at[0]),
        begin_local(gain_in, gain, sem_l.at[1]),
        begin_local(bias_in, bias, sem_l.at[2]),
    ]
    homes = [
        (w_qkv.at[pl.ds(HD, 2 * HD)], wkv.at[mate], wkv.at[mate]),
        (w_qkv.at[pl.ds(0, HD)], wq.at[mate], wq.at[mate]),
        (w_out, wo.at[0, mate], wo.at[0, mate]),
        (w_gate, wgv.at[0], wgv.at[1]),
        (w_value, wgv.at[2], wgv.at[3]),
        (w_down, wdown.at[0], wdown.at[1]),
    ]
    groups = (0, 0, 1, 2, 2, 3)

    def fetch(first, last):
        for index in range(first, last):
            begin_local(homes[index][0], homes[index][1], sem_w.at[groups[index]])

    def share(first, last, kind):
        for index in range(first, last):
            begin(homes[index][0], homes[index][2], kind, sem_wr.at[groups[index]], sibling)

    def wait_weights(group, whole):
        pltpu.make_async_copy(whole, whole, sem_w.at[group]).wait()
        remote(whole, whole, sem_s.at[SHARE], sem_wr.at[group], sibling).wait_recv()

    fetch(0, 3)
    local[0].wait()
    pl.semaphore_wait(barrier, 12)

    def quarter(slot, index):
        return rows_far.at[slot, index // 2, pl.ds(2 * (index % 2), 2)]

    across = [
        begin(rows_in.at[me, pl.ds(2 * index, 2)], quarter(me, index), ACROSS, sem_pr.at[index], plane(4))
        for index in range(4)
    ]
    for distance in range(7, 0, -1):
        begin(rows_in.at[me], rows_in.at[me], NEAR, sem_xr.at[distance], chip(distance))
    share(0, 3, SHARE)
    fetch(3, 6)
    share(3, 6, SHARE_FFN)

    def spread_out(rows):
        for distance in range(7, 0, -1):
            begin(w_out.at[rows], wo.at[distance, mate, rows], OUT, sem_or.at[distance], chip(distance))

    def near_copy(distance):
        block = rows_in.at[lax.bitwise_xor(me, distance)]
        return remote(block, block, sem_s.at[NEAR], sem_xr.at[distance], chip(distance))

    def far_copy(part, distance):
        block = rows_far.at[lax.bitwise_xor(me, distance), part]
        return remote(block, block, sem_s.at[FAR], sem_yr.at[part, distance], chip(distance))

    def near_norm(distance):
        slot = lax.bitwise_xor(me, distance)
        for part in range(2):
            rows = rows_in[slot, pl.ds(4 * part, 4)].astype(F32).reshape(16, width)
            stream[part, slot] = rows.astype(BF16)
            tokens[0, part, slot] = norm_rows(rows, gain[0:1, :], bias[0:1, :])

    def near_step(distance, carry):
        near_copy(distance).wait_recv()
        near_norm(distance)
        return carry

    for copy in local[1:]:
        copy.wait()
    near_norm(0)
    for index in range(4):
        across[index].wait_recv()
        for distance in range(7, 0, -1):
            mine = quarter(me, index)
            begin(mine, mine, FAR, sem_yr.at[index // 2, distance], chip(distance))
    spread_out(pl.ds(0, 16))
    lax.fori_loop(1, 8, near_step, 0)
    wait_weights(0, w_qkv)

    scale = HD ** (-0.5) * math.log2(math.e)

    def project(which, part):
        piece = tokens[which, part].reshape(128, width)
        place = pl.ds(128 * part, 128)
        keys[4 * which, core, place] = dot(piece, wkv[0], 1, 1).astype(BF16)
        query[0:HD, pl.ds(256 * which + 128 * part, 128)] = (dot(wq[0], piece, 1, 1) * scale).astype(BF16)

    def send_sibling(slot):
        block = keys.at[slot, core]
        begin(block, block, SIBLING, sem_gr.at[slot // 4], sibling)

    def from_sibling(group):
        blocks = keys.at[pl.ds(4 * group, 4), 1 - core]
        remote(blocks, blocks, sem_s.at[SIBLING], sem_gr.at[group], sibling).wait_recv()

    def from_plane(slot):
        block = keys.at[slot, core]
        remote(block, block, sem_s.at[NEAR_KEYS], sem_zr.at[slot], plane(4)).wait_recv()

    for part in range(2):
        project(0, part)
    for distance in range(3, 0, -1):
        begin(keys.at[0, core], keys.at[distance, core], NEAR_KEYS, sem_zr.at[distance], plane(distance))
    send_sibling(0)
    query[HD:, :] = jnp.zeros((HD, 512), BF16)

    def far_step(distance, part):
        @pl.when(distance >= 1)
        def _():
            far_copy(part, distance).wait_recv()

        slot = lax.bitwise_xor(me, distance)
        rows = rows_far[slot, part].astype(F32).reshape(16, width)
        tokens[1, part, slot] = norm_rows(rows, gain[0:1, :], bias[0:1, :])
        return part

    for part in range(2):
        lax.fori_loop(0, 8, far_step, part)
        project(1, part)
        place = pl.ds(128 * part, 128)
        for distance in range(3, 0, -1):
            begin(
                keys.at[4, core, place], keys.at[4 + distance, core, place],
                FAR_KEYS, sem_zr.at[4 + distance], plane(distance),
            )
    send_sibling(4)
    spread_out(pl.ds(16, 48))

    def scored(block, first, count):
        return dot(block, query[:, first : first + count], 1, 0)

    def summed_values(block, probs):
        lanes = lax.broadcasted_iota(jnp.int32, block.shape, 1)
        return dot(jnp.where(lanes < HD, jnp.ones_like(block), block), probs, 0, 0)

    def fold(block, first, count):
        scores = scored(block, first, count)
        old = top[:, first : first + count]
        new = jnp.maximum(old, jnp.max(scores, axis=0, keepdims=True))
        probs = jnp.exp2(scores - new).astype(BF16)
        accum[:, first : first + count] = accum[:, first : first + count] * jnp.exp2(old - new) + summed_values(block, probs)
        top[:, first : first + count] = new

    def attended_by(first):
        return (accum[HD:, first : first + 256] / accum[0:1, first : first + 256]).astype(BF16)

    for near in range(1, 4):
        from_plane(near)
        send_sibling(near)
    wait_weights(2, wgv.at[pl.ds(0, 2)])
    for index in range(4):
        wgv_t[:, pl.ds(320 * index, 320)] = wgv[index].T
    from_sibling(0)
    block = keys[0:4].reshape(2048, 2 * HD)
    scores = scored(block, 0, 512)
    first_top = jnp.max(scores, axis=0, keepdims=True)
    top[...] = first_top
    accum[...] = summed_values(block, jnp.exp2(scores - first_top).astype(BF16))
    for far in range(5, 8):
        from_plane(far)
        send_sibling(far)
    fold(keys[pl.ds(4, 4), core].reshape(1024, 2 * HD), 256, 256)
    from_sibling(1)
    fold(keys[pl.ds(4, 4), 1 - core].reshape(1024, 2 * HD), 256, 256)
    attended_other[...] = attended_by(256)
    returned = begin(attended_other, attended.at[0, pl.ds(HD, HD)], RETURN, sem_pr.at[4], plane(4))
    fold(keys[4:8].reshape(2048, 2 * HD), 0, 256)

    attended[0, 0:HD] = attended_by(0)
    def spread_heads(group, block):
        for distance in range(7, 0, -1):
            begin(attended.at[0, *block], attended.at[distance, *block], HEADS, sem_ar.at[group], chip(distance))

    def wait_heads(group, block):
        blocks = attended.at[pl.ds(1, 7), *block]
        remote(blocks, blocks, sem_s.at[HEADS], sem_ar.at[group], sibling).wait_recv()

    first_heads = (pl.ds(0, HD), pl.ds(0, 256))

    def later_heads(part):
        return pl.ds(HD, HD), pl.ds(pl.multiple_of(128 * part, 128), 128)

    spread_heads(0, first_heads)
    wait_weights(1, w_out)
    for distance in range(7, 0, -1):
        block = wo.at[distance, mate]
        remote(block, block, sem_s.at[OUT], sem_or.at[distance], chip(distance)).wait_recv()
        begin(block, block, FORWARD, sem_or.at[0], sibling)
    returned.wait_recv()
    for part in range(2):
        spread_heads(1 + part, later_heads(part))
    blocks = wo.at[pl.ds(1, 7), 1 - mate]
    remote(blocks, blocks, sem_s.at[FORWARD], sem_or.at[0], sibling).wait_recv()
    wait_heads(0, first_heads)

    heads = attended[:, :HD].reshape(8 * HD, 256)
    attn_sum[...] = dot(heads, wo[:, 0].reshape(8 * HD, width), 0, 0).reshape(attn_sum.shape)
    wait_weights(3, w_down)

    units = wdown.shape[0] * wdown.shape[1]

    def piece(slot, part):
        return remote(
            partial.at[part, lax.bitwise_xor(me, slot)], summed.at[slot, part],
            sem_s.at[PIECE], sem_cr.at[slot], chip(slot),
        )

    def feed(part, carry):
        wait_heads(1 + part, later_heads(part))
        heads = attended[:, HD:, pl.ds(pl.multiple_of(128 * part, 128), 128)].reshape(8 * HD, 128)
        added = attn_sum[part] + dot(heads, wo[:, 1].reshape(8 * HD, width), 0, 0)
        rounded = (stream[part].reshape(128, width).astype(F32) + added).astype(BF16)
        stream[part] = rounded.reshape(8, 16, width)
        rows = rounded.astype(F32)
        normed = norm_rows(rows, gain[1:2, :], bias[1:2, :])
        sums = dot(normed, wgv_t[...], 1, 0)
        gate, value = sums[:, :units], sums[:, units:]
        hidden = (value * (gate * (lax.erf(gate * (0.5**0.5)) + 1.0) * 0.5)).astype(BF16)
        terms = dot(hidden, wdown[...].reshape(units, width), 1, 0)
        partial[part] = terms.astype(BF16).reshape(8, 16, width)
        for distance in range(7, 0, -1):
            piece(distance, part).start()
        return carry

    lax.fori_loop(0, 2, feed, 0)
    total = stream[:, me].astype(F32) + partial[:, me].astype(F32)
    for distance in range(1, 8):
        block = summed.at[distance]
        remote(block, block, sem_s.at[PIECE], sem_cr.at[distance], sibling).wait_recv()
        total += summed[distance].astype(F32)
    result[...] = total.reshape(8, 4, width).astype(BF16)

    seven = pl.ds(0, 7)
    three = keys.at[pl.ds(0, 3), 0]
    for kind, sent in (
        (NEAR, rows_in.at[seven]),
        (ACROSS, rows_far.at[0]),
        (FAR, rows_far.at[seven]),
        (SHARE, wkv),
        (SHARE_FFN, wgv.at[pl.ds(0, 3)]),
        (NEAR_KEYS, three),
        (FAR_KEYS, three),
        (SIBLING, keys.at[:, 0]),
        (OUT, wo.at[seven, 0]),
        (FORWARD, wo.at[seven, 0]),
        (RETURN, attended_other),
        (HEADS, attended.at[seven]),
        (PIECE, summed.at[seven]),
    ):
        remote(sent, sent, sem_s.at[kind], sem_pr.at[0], sibling).wait_send()


def per_device(latent, ln_gain, ln_bias, w_qkv, w_out, w_gate, w_value, w_down):
    width = latent.shape[-1]
    own_units = w_gate.shape[2]
    vmem, anywhere = pl.BlockSpec(memory_space=pltpu.VMEM), pl.BlockSpec(memory_space=pl.ANY)
    dma = pltpu.SemaphoreType.DMA
    return pl.pallas_call(
        block_kernel,
        out_shape=pltpu.VMEM(latent.shape, BF16),
        in_specs=[anywhere] * 8,
        out_specs=vmem,
        scratch_shapes=[
            pltpu.VMEM((8, *latent.shape), BF16),
            pltpu.VMEM((8, 2, 4, *latent.shape[1:]), BF16),
            pltpu.VMEM((2, width), F32),
            pltpu.VMEM((2, width), F32),
            pltpu.VMEM((2, 2, 8, 16, width), BF16),
            pltpu.VMEM((2, 8, 16, width), BF16),
            pltpu.VMEM((2, 8, 16, width), BF16),
            pltpu.VMEM((8, 2, 16, width), BF16),
            pltpu.VMEM((8, 2, 256, 2 * HD), BF16),
            pltpu.VMEM((2 * HD, 512), BF16),
            pltpu.VMEM((2, 2 * HD, width), BF16),
            pltpu.VMEM((2, HD, width), BF16),
            pltpu.VMEM((8, 2, HD, width), BF16),
            pltpu.VMEM((4, own_units, width), BF16),
            pltpu.VMEM((width, 4 * own_units), BF16),
            pltpu.VMEM((2, own_units, width), BF16),
            pltpu.VMEM((1, 512), F32),
            pltpu.VMEM((2 * HD, 512), F32),
            pltpu.VMEM((2, 128, width), F32),
            pltpu.VMEM((8, 2 * HD, 256), BF16),
            pltpu.VMEM((HD, 256), BF16),
            dma((3,)),
            dma((4,)),
            dma((4,)),
            dma((8,)),
            dma((8,)),
            dma((2, 8)),
            dma((3,)),
            dma((8,)),
            dma((2,)),
            dma((8,)),
            dma((5,)),
            dma((14,)),
        ],
        compiler_params=pltpu.CompilerParams(
            collective_id=0, has_side_effects=True, vmem_limit_bytes=56 * 2**20
        ),
        name="transformer_block",
    )(
        latent,
        ln_gain[0],
        ln_bias[0],
        w_qkv[0].transpose(1, 0, 2).reshape(3 * HD, width),
        w_out[0],
        w_gate[0].T,
        w_value[0].T,
        w_down[0],
    )


def solution(mesh):
    return jax.shard_map(
        per_device,
        mesh=mesh,
        in_specs=(
            P("rows", "cols", None),
            P(),
            P(),
            P(None, "cols", None, None),
            P(None, "cols", None),
            P(None, None, "cols"),
            P(None, None, "cols"),
            P(None, "cols", None),
        ),
        out_specs=P("rows", "cols", None),
        check_vma=False,
    )
```

```python
import math

import jax
import jax.numpy as jnp
from jax import lax
from jax.experimental import pallas as pl
from jax.experimental.pallas import tpu as pltpu
from jax.sharding import PartitionSpec as P

HD = 64
MESH = pl.DeviceIdType.MESH
F32, BF16 = jnp.float32, jnp.bfloat16


def norm_rows(values, gain, bias):
    row_mean = jnp.mean(values, axis=-1, keepdims=True)
    centred = values - row_mean
    row_var = jnp.mean(centred * centred, axis=-1, keepdims=True)
    return (centred * lax.rsqrt(row_var + 1e-05) * gain + bias).astype(BF16)


def dot(left, right, left_dim, right_dim):
    return lax.dot_general(
        left, right, (((left_dim,), (right_dim,)), ((), ())), preferred_element_type=F32
    )


def block_kernel(
    latent, gain_in, bias_in, w_qkv, w_out, w_gate, w_value, w_down, result,
    rows_in, rows_far, gain, bias, tokens, stream, partial, summed, keys, query,
    wkv, wq, wo, wgv, wgv_t, wdown, top, accum, attn_sum, attended, attended_other,
    sem_l, sem_w, sem_wr, sem_or, sem_xr, sem_yr, sem_ar, sem_zr, sem_gr, sem_cr, sem_pr, sem_s,
):
    row, col = lax.axis_index("rows"), lax.axis_index("cols")
    core, me = col % 2, col // 2
    mate = lax.bitwise_xor(core, row % 8 // 4)
    sibling = (row, col + 1 - 2 * core)
    width = gain.shape[1]

    def chip(distance):
        return (row, lax.bitwise_xor(col, 2 * distance))

    def plane(distance):
        return (lax.bitwise_xor(row, distance), col)

    def remote(src, dst, send, recv, device):
        return pltpu.make_async_remote_copy(
            src_ref=src, dst_ref=dst, send_sem=send, recv_sem=recv, device_id=device, device_id_type=MESH
        )

    NEAR, ACROSS, FAR, SHARE, SHARE_FFN, NEAR_KEYS, FAR_KEYS, SIBLING, OUT, FORWARD, RETURN, HEADS, PIECE, EXCHANGE = range(14)

    def begin(src, dst, kind, recv, device):
        copy = remote(src, dst, sem_s.at[kind], recv, device)
        copy.start()
        return copy

    barrier = pltpu.get_barrier_semaphore()
    pl.semaphore_signal(barrier, inc=1, device_id=plane(4), device_id_type=MESH)
    for distance in range(7, 0, -1):
        pl.semaphore_signal(barrier, inc=1, device_id=chip(distance), device_id_type=MESH)
    for distance in range(1, 4):
        pl.semaphore_signal(barrier, inc=1, device_id=plane(distance), device_id_type=MESH)
    pl.semaphore_signal(barrier, inc=1, device_id=sibling, device_id_type=MESH)

    def begin_local(src, dst, sem):
        copy = pltpu.make_async_copy(src, dst, sem)
        copy.start()
        return copy

    local = [
        begin_local(latent, rows_in.at[me], sem_l.at[0]),
        begin_local(gain_in, gain, sem_l.at[1]),
        begin_local(bias_in, bias, sem_l.at[2]),
    ]
    homes = [
        (w_qkv.at[pl.ds(HD, 2 * HD)], wkv.at[mate], wkv.at[mate]),
        (w_qkv.at[pl.ds(0, HD)], wq.at[mate], wq.at[mate]),
        (w_out, wo.at[0, mate], wo.at[0, mate]),
        (w_gate, wgv.at[0], wgv.at[1]),
        (w_value, wgv.at[2], wgv.at[3]),
        (w_down, wdown.at[0], wdown.at[1]),
    ]
    groups = (0, 0, 1, 2, 2, 3)

    def fetch(first, last):
        for index in range(first, last):
            begin_local(homes[index][0], homes[index][1], sem_w.at[groups[index]])

    def share(first, last, kind):
        for index in range(first, last):
            begin(homes[index][0], homes[index][2], kind, sem_wr.at[groups[index]], sibling)

    def wait_weights(group, whole):
        pltpu.make_async_copy(whole, whole, sem_w.at[group]).wait()
        remote(whole, whole, sem_s.at[SHARE], sem_wr.at[group], sibling).wait_recv()

    fetch(0, 3)
    local[0].wait()
    pl.semaphore_wait(barrier, 12)

    def quarter(slot, index):
        return rows_far.at[slot, index // 2, pl.ds(2 * (index % 2), 2)]

    across = [
        begin(rows_in.at[me, pl.ds(2 * index, 2)], quarter(me, index), ACROSS, sem_pr.at[index], plane(4))
        for index in range(4)
    ]
    for distance in range(7, 0, -1):
        begin(rows_in.at[me], rows_in.at[me], NEAR, sem_xr.at[distance], chip(distance))
    share(0, 3, SHARE)
    fetch(3, 6)
    share(3, 6, SHARE_FFN)

    def spread_out(rows):
        for distance in range(7, 0, -1):
            begin(w_out.at[rows], wo.at[distance, mate, rows], OUT, sem_or.at[distance], chip(distance))

    def near_copy(distance):
        block = rows_in.at[lax.bitwise_xor(me, distance)]
        return remote(block, block, sem_s.at[NEAR], sem_xr.at[distance], chip(distance))

    def far_copy(part, distance):
        block = rows_far.at[lax.bitwise_xor(me, distance), part]
        return remote(block, block, sem_s.at[FAR], sem_yr.at[part, distance], chip(distance))

    def near_norm(distance):
        slot = lax.bitwise_xor(me, distance)
        for part in range(2):
            rows = rows_in[slot, pl.ds(4 * part, 4)].astype(F32).reshape(16, width)
            stream[part, slot] = rows.astype(BF16)
            tokens[0, part, slot] = norm_rows(rows, gain[0:1, :], bias[0:1, :])

    def near_step(distance, carry):
        near_copy(distance).wait_recv()
        near_norm(distance)
        return carry

    for copy in local[1:]:
        copy.wait()
    near_norm(0)
    for index in range(4):
        across[index].wait_recv()
        for distance in range(7, 0, -1):
            mine = quarter(me, index)
            begin(mine, mine, FAR, sem_yr.at[index // 2, distance], chip(distance))
    lax.fori_loop(1, 8, near_step, 0)
    spread_out(pl.ds(0, 16))
    wait_weights(0, w_qkv)

    scale = HD ** (-0.5) * math.log2(math.e)

    def project(which, part):
        piece = tokens[which, part].reshape(128, width)
        place = pl.ds(128 * part, 128)
        keys[4 * which, core, place] = dot(piece, wkv[0], 1, 1).astype(BF16)
        query[0:HD, pl.ds(256 * which + 128 * part, 128)] = (dot(wq[0], piece, 1, 1) * scale).astype(BF16)

    def send_sibling(slot):
        block = keys.at[slot, core]
        begin(block, block, SIBLING, sem_gr.at[slot // 4], sibling)

    def from_sibling(group):
        blocks = keys.at[pl.ds(4 * group, 4), 1 - core]
        remote(blocks, blocks, sem_s.at[SIBLING], sem_gr.at[group], sibling).wait_recv()

    def from_plane(slot):
        block = keys.at[slot, core]
        remote(block, block, sem_s.at[NEAR_KEYS], sem_zr.at[slot], plane(4)).wait_recv()

    for part in range(2):
        project(0, part)
    for distance in range(3, 0, -1):
        begin(keys.at[0, core], keys.at[distance, core], NEAR_KEYS, sem_zr.at[distance], plane(distance))
    send_sibling(0)
    query[HD:, :] = jnp.zeros((HD, 512), BF16)

    def far_step(distance, part):
        @pl.when(distance >= 1)
        def _():
            far_copy(part, distance).wait_recv()

        slot = lax.bitwise_xor(me, distance)
        rows = rows_far[slot, part].astype(F32).reshape(16, width)
        tokens[1, part, slot] = norm_rows(rows, gain[0:1, :], bias[0:1, :])
        return part

    for part in range(2):
        lax.fori_loop(0, 8, far_step, part)
        project(1, part)
        place = pl.ds(128 * part, 128)
        for distance in range(3, 0, -1):
            begin(
                keys.at[4, core, place], keys.at[4 + distance, core, place],
                FAR_KEYS, sem_zr.at[4 + distance], plane(distance),
            )
    send_sibling(4)
    spread_out(pl.ds(16, 48))

    def scored(block, first, count):
        return dot(block, query[:, first : first + count], 1, 0)

    def summed_values(block, probs):
        lanes = lax.broadcasted_iota(jnp.int32, block.shape, 1)
        return dot(jnp.where(lanes < HD, jnp.ones_like(block), block), probs, 0, 0)

    def fold(block, first, count):
        scores = scored(block, first, count)
        old = top[:, first : first + count]
        new = jnp.maximum(old, jnp.max(scores, axis=0, keepdims=True))
        probs = jnp.exp2(scores - new).astype(BF16)
        accum[:, first : first + count] = accum[:, first : first + count] * jnp.exp2(old - new) + summed_values(block, probs)
        top[:, first : first + count] = new

    def attended_by(first):
        return (accum[HD:, first : first + 256] / accum[0:1, first : first + 256]).astype(BF16)

    for near in range(1, 4):
        from_plane(near)
        send_sibling(near)
    wait_weights(2, wgv.at[pl.ds(0, 2)])
    for index in range(4):
        wgv_t[:, pl.ds(320 * index, 320)] = wgv[index].T
    from_sibling(0)
    block = keys[0:4].reshape(2048, 2 * HD)
    scores = scored(block, 0, 512)
    first_top = jnp.max(scores, axis=0, keepdims=True)
    top[...] = first_top
    accum[...] = summed_values(block, jnp.exp2(scores - first_top).astype(BF16))
    for far in range(5, 8):
        from_plane(far)
        send_sibling(far)
    fold(keys[pl.ds(4, 4), core].reshape(1024, 2 * HD), 256, 256)
    from_sibling(1)
    fold(keys[pl.ds(4, 4), 1 - core].reshape(1024, 2 * HD), 256, 256)
    attended_other[...] = attended_by(256)
    returned = []
    for part in range(2):
        place = pl.ds(128 * part, 128)
        returned.append(
            begin(
                attended_other.at[:, place], attended.at[0, pl.ds(HD, HD), place],
                RETURN, sem_pr.at[4 + part], plane(4),
            )
        )
    fold(keys[4:8].reshape(2048, 2 * HD), 0, 256)

    attended[0, 0:HD] = attended_by(0)
    def spread_heads(group, block):
        for distance in range(7, 0, -1):
            begin(attended.at[0, *block], attended.at[distance, *block], HEADS, sem_ar.at[group], chip(distance))

    def wait_heads(group, block):
        blocks = attended.at[pl.ds(1, 7), *block]
        remote(blocks, blocks, sem_s.at[HEADS], sem_ar.at[group], sibling).wait_recv()

    first_heads = (pl.ds(0, HD), pl.ds(0, 256))

    def later_heads(part):
        return pl.ds(HD, HD), pl.ds(pl.multiple_of(128 * part, 128), 128)

    spread_heads(0, first_heads)
    wait_weights(1, w_out)
    for distance in range(7, 0, -1):
        block = wo.at[distance, mate]
        remote(block, block, sem_s.at[OUT], sem_or.at[distance], chip(distance)).wait_recv()
        begin(block, block, FORWARD, sem_or.at[0], sibling)
    for part in range(2):
        returned[part].wait_recv()
        spread_heads(1 + part, later_heads(part))
    blocks = wo.at[pl.ds(1, 7), 1 - mate]
    remote(blocks, blocks, sem_s.at[FORWARD], sem_or.at[0], sibling).wait_recv()
    wait_heads(0, first_heads)

    heads = attended[:, :HD].reshape(8 * HD, 256)
    attn_sum[...] = dot(heads, wo[:, 0].reshape(8 * HD, width), 0, 0).reshape(attn_sum.shape)
    wait_weights(3, w_down)

    units = wdown.shape[0] * wdown.shape[1]

    def piece(slot, part):
        return remote(
            partial.at[part, lax.bitwise_xor(me, slot)], summed.at[slot, part],
            sem_s.at[PIECE], sem_cr.at[slot], chip(slot),
        )

    def feed(part, carry):
        wait_heads(1 + part, later_heads(part))
        heads = attended[:, HD:, pl.ds(pl.multiple_of(128 * part, 128), 128)].reshape(8 * HD, 128)
        added = attn_sum[part] + dot(heads, wo[:, 1].reshape(8 * HD, width), 0, 0)
        rounded = (stream[part].reshape(128, width).astype(F32) + added).astype(BF16)
        stream[part] = rounded.reshape(8, 16, width)
        rows = rounded.astype(F32)
        normed = norm_rows(rows, gain[1:2, :], bias[1:2, :])
        sums = dot(normed, wgv_t[...], 1, 0)
        gate, value = sums[:, :units], sums[:, units:]
        hidden = (value * (gate * (lax.erf(gate * (0.5**0.5)) + 1.0) * 0.5)).astype(BF16)
        terms = dot(hidden, wdown[...].reshape(units, width), 1, 0)
        partial[part] = terms.astype(BF16).reshape(8, 16, width)
        for distance in range(7, 0, -1):
            piece(distance, part).start()
        return carry

    lax.fori_loop(0, 2, feed, 0)
    total = stream[:, me].astype(F32) + partial[:, me].astype(F32)
    for distance in range(1, 8):
        block = summed.at[distance]
        remote(block, block, sem_s.at[PIECE], sem_cr.at[distance], sibling).wait_recv()
        total += summed[distance].astype(F32)
    result[...] = total.reshape(8, 4, width).astype(BF16)

    seven = pl.ds(0, 7)
    three = keys.at[pl.ds(0, 3), 0]
    for kind, sent in (
        (NEAR, rows_in.at[seven]),
        (ACROSS, rows_far.at[0]),
        (FAR, rows_far.at[seven]),
        (SHARE, wkv),
        (SHARE_FFN, wgv.at[pl.ds(0, 3)]),
        (NEAR_KEYS, three),
        (FAR_KEYS, three),
        (SIBLING, keys.at[:, 0]),
        (OUT, wo.at[seven, 0]),
        (FORWARD, wo.at[seven, 0]),
        (RETURN, attended_other),
        (HEADS, attended.at[seven]),
        (PIECE, summed.at[seven]),
    ):
        remote(sent, sent, sem_s.at[kind], sem_pr.at[0], sibling).wait_send()


def per_device(latent, ln_gain, ln_bias, w_qkv, w_out, w_gate, w_value, w_down):
    width = latent.shape[-1]
    own_units = w_gate.shape[2]
    vmem, anywhere = pl.BlockSpec(memory_space=pltpu.VMEM), pl.BlockSpec(memory_space=pl.ANY)
    dma = pltpu.SemaphoreType.DMA
    return pl.pallas_call(
        block_kernel,
        out_shape=pltpu.VMEM(latent.shape, BF16),
        in_specs=[anywhere] * 8,
        out_specs=vmem,
        scratch_shapes=[
            pltpu.VMEM((8, *latent.shape), BF16),
            pltpu.VMEM((8, 2, 4, *latent.shape[1:]), BF16),
            pltpu.VMEM((2, width), F32),
            pltpu.VMEM((2, width), F32),
            pltpu.VMEM((2, 2, 8, 16, width), BF16),
            pltpu.VMEM((2, 8, 16, width), BF16),
            pltpu.VMEM((2, 8, 16, width), BF16),
            pltpu.VMEM((8, 2, 16, width), BF16),
            pltpu.VMEM((8, 2, 256, 2 * HD), BF16),
            pltpu.VMEM((2 * HD, 512), BF16),
            pltpu.VMEM((2, 2 * HD, width), BF16),
            pltpu.VMEM((2, HD, width), BF16),
            pltpu.VMEM((8, 2, HD, width), BF16),
            pltpu.VMEM((4, own_units, width), BF16),
            pltpu.VMEM((width, 4 * own_units), BF16),
            pltpu.VMEM((2, own_units, width), BF16),
            pltpu.VMEM((1, 512), F32),
            pltpu.VMEM((2 * HD, 512), F32),
            pltpu.VMEM((2, 128, width), F32),
            pltpu.VMEM((8, 2 * HD, 256), BF16),
            pltpu.VMEM((HD, 256), BF16),
            dma((3,)),
            dma((4,)),
            dma((4,)),
            dma((8,)),
            dma((8,)),
            dma((2, 8)),
            dma((3,)),
            dma((8,)),
            dma((2,)),
            dma((8,)),
            dma((6,)),
            dma((14,)),
        ],
        compiler_params=pltpu.CompilerParams(
            collective_id=0, has_side_effects=True, vmem_limit_bytes=56 * 2**20
        ),
        name="transformer_block",
    )(
        latent,
        ln_gain[0],
        ln_bias[0],
        w_qkv[0].transpose(1, 0, 2).reshape(3 * HD, width),
        w_out[0],
        w_gate[0].T,
        w_value[0].T,
        w_down[0],
    )


def solution(mesh):
    return jax.shard_map(
        per_device,
        mesh=mesh,
        in_specs=(
            P("rows", "cols", None),
            P(),
            P(),
            P(None, "cols", None, None),
            P(None, "cols", None),
            P(None, None, "cols"),
            P(None, None, "cols"),
            P(None, "cols", None),
        ),
        out_specs=P("rows", "cols", None),
        check_vma=False,
    )
```
